256 devices in a mesh: group: 8 (over y, core), local: 32 (over z, x).
Axes of the slice: x: 4, y: 4, z: 8, core: 2. Of those that a mesh axis runs over, the one named last changes fastest.
Arguments:
- tokens: bfloat16 [6144, 2048], P(('group', 'local')), may hold values from -6 to 6
- out_grad: bfloat16 [6144, 2048], P(('group', 'local')), may hold values from -0.59765625 to 0.59765625
- experts: int32 [6144, 8], P(('group', 'local')), may hold values from 0 to 127, as said below
- gate_values: float32 [6144, 8], P(('group', 'local')), may hold values from 0.02 to 0.5
- slot_map: int32 [8, 32], replicated, may hold values from 0 to 31, each once within a row
- gate_weight: bfloat16 [256, 2048, 384], P(('group', 'local')), may hold values from -0.125 to 0.125
- up_weight: bfloat16 [256, 2048, 384], P(('group', 'local')), may hold values from -0.125 to 0.125
- down_weight: bfloat16 [256, 384, 2048], P(('group', 'local')), may hold values from -0.21875 to 0.21875
Outputs:
- layer_out: bfloat16 [6144, 2048], P(('group', 'local'))
- token_grad: bfloat16 [6144, 2048], P(('group', 'local'))
- gate_grad: float32 [6144, 8], P(('group', 'local'))
- gate_weight_grad: bfloat16 [256, 2048, 384], P(('group', 'local'))
- up_weight_grad: bfloat16 [256, 2048, 384], P(('group', 'local'))
- down_weight_grad: bfloat16 [256, 384, 2048], P(('group', 'local'))
The draws below stay inside these ranges and needn't reach their ends.
Inputs may be any that keep to these rules, and one draw needn't show every extreme that they name: A token names 8 different experts, all within at most 4 groups of 16 consecutive experts; the tokens of one device name each expert at most 3 times, and in every draw some expert is named exactly 3 times by the tokens of every device. `slot_map`: each row is a permutation; in group g the two devices whose entries are 2 k and 2 k + 1 hold expert g * 16 + k.
All inputs are finite; a program needn't handle non-finite values.
Results may differ from the reference program's by a relative error of at most 0.0064.
Values may be sent and summed in bfloat16 or wider, within the bound.
No kernel may reach another device: no remote copies, remote signals or barrier semaphores. Data moves between devices by JAX's collectives and lax.ppermute only.
A program may use at most 128 MiB of HBM per device.

```python
import math
import jax
import jax.numpy as jnp
from jax import lax

D = 2048
FF = 768
TOP = 8
GROUP_MAX = 4
TOK_DEV = 24
EXPERTS = 128
EPG = 16
FFH = 384
CAP = 3
TOKENS = 6144
N_GROUP = 8
N_LOCAL = 32


def draw_experts(key, part):
    key = jax.random.fold_in(key, 7)
    blocks = TOKENS // TOK_DEV
    experts_all = N_GROUP * N_LOCAL // 2
    per_group = experts_all // N_GROUP
    capacity = 2 * TOK_DEV * TOP // experts_all
    key_favour, key_hot, key_blocks = jax.random.split(key, 3)
    favour = jax.random.randint(key_favour, (experts_all,), 0, 4) * 256
    hottest = jax.random.randint(key_hot, (), 0, experts_all)
    expert_ids = jnp.arange(experts_all, dtype=jnp.int32)
    group_ids = jnp.arange(N_GROUP, dtype=jnp.int32)
    last_expert = experts_all - 1

    def one_block(block_key):
        key_order, key_group, key_expert = jax.random.split(block_key, 3)
        order = jax.random.permutation(key_order, TOK_DEV)
        forced = order < capacity
        tail = order == TOK_DEV - 1
        noise_group = jax.random.randint(key_group, (TOK_DEV, N_GROUP), 0, 1024)
        noise_expert = jax.random.randint(key_expert, (TOK_DEV, experts_all), 0, 1024)

        def step(counts, inputs):
            must, last_one, group_noise, expert_noise = inputs
            allowed = (counts < capacity) & ((expert_ids != hottest) | must)
            room = jnp.sum(allowed.reshape(N_GROUP, per_group).astype(jnp.int32), axis=1)
            hot_group = (group_ids == hottest // per_group) & must
            tail_group = (group_ids == last_expert // per_group) & last_one
            group_score = (room * 1024 + group_noise) * N_GROUP + group_ids + jnp.where(hot_group, 1 << 26, 0)
            group_score = group_score + jnp.where(tail_group, 1 << 25, 0)
            unused, top_groups = lax.top_k(group_score, GROUP_MAX)
            chosen = jnp.any(top_groups[:, None] == group_ids[None, :], axis=0)
            in_group = chosen[expert_ids // per_group]
            expert_score = (favour + expert_noise) * experts_all + expert_ids
            expert_score = expert_score + jnp.where((expert_ids == hottest) & must, 1 << 28, 0)
            expert_score = expert_score + jnp.where((expert_ids == last_expert) & last_one, 1 << 27, 0)
            expert_score = jnp.where(allowed & in_group, expert_score, -1)
            unused_scores, choice_ids = lax.top_k(expert_score, TOP)
            counts = counts + jnp.sum((choice_ids[:, None] == expert_ids[None, :]).astype(jnp.int32), axis=0)
            return (counts, choice_ids.astype(jnp.int32))
        final, chosen_ids = lax.scan(step, jnp.zeros((experts_all,), jnp.int32), (forced, tail, noise_group, noise_expert))
        return chosen_ids
    block_keys = jax.random.split(key_blocks, blocks)
    return jax.vmap(one_block)(block_keys).reshape(TOKENS, TOP).astype(jnp.int32)


def block_scale(stream_key, shape, pieces, low, high):
    factor_of, own = 1.0, jax.random.fold_in(stream_key, 6)
    for axis_at, parts in pieces:
        heights = jnp.exp(jax.random.uniform(jax.random.fold_in(own, axis_at), (parts,), jnp.float32, low / len(pieces), high / len(pieces)))
        factor_of = factor_of * jnp.repeat(heights, shape[axis_at] // parts).reshape([-1 if axis == axis_at else 1 for axis in range(len(shape))])
    return factor_of


def normal_values(stream_key, dims, deviation, limit, shards=(), kind=jnp.bfloat16):
    drawn = jax.random.normal(stream_key, dims, jnp.float32) * deviation
    if len(shards) > 0:
        drawn = block_scale(stream_key, dims, shards, -0.22, 0.18) * drawn
    return jnp.clip(drawn, min=-limit, max=limit).astype(kind)


def setup_inputs(seed: int = 0) -> dict:
    key_list = jax.random.split(jax.random.key(seed), 9)
    tokens = normal_values(key_list[0], (TOKENS, D), 1.0, 6.0, ((0, 256),))
    out_grad = normal_values(key_list[1], (TOKENS, D), 0.1, 0.59765625, ((0, 256),))
    experts = draw_experts(jax.random.fold_in(key_list[8], 71), 0)
    gate_values = jnp.clip(jnp.exp(math.log(0.5) - 3.218876 * jax.random.uniform(key_list[3], (TOKENS, TOP), jnp.float32) ** block_scale(key_list[3], (TOKENS, TOP), ((0, 256),), -0.2, 0.2)), 0.02, 0.5)
    slot_map = jax.vmap(lambda own: jax.random.permutation(own, N_LOCAL))(jax.random.split(key_list[4], N_GROUP)).reshape((N_GROUP, N_LOCAL)).astype(jnp.int32)
    gate_weight = normal_values(key_list[5], (N_GROUP * N_LOCAL, D, FFH), D ** -0.5, 0.125, ((0, 256),))
    up_weight = normal_values(key_list[6], (N_GROUP * N_LOCAL, D, FFH), D ** -0.5, 0.125, ((0, 256),))
    down_weight = normal_values(key_list[7], (N_GROUP * N_LOCAL, FFH, D), FF ** -0.5, 0.21875, ((0, 256),))
    return dict(tokens=tokens, out_grad=out_grad, experts=experts, gate_values=gate_values, slot_map=slot_map, gate_weight=gate_weight, up_weight=up_weight, down_weight=down_weight)


def expert_pass(slot_rows, scaled, gate_slab, up_slab, down_slab):
    gate_pre = jnp.dot(slot_rows, gate_slab, preferred_element_type=jnp.float32)
    up_pre = jnp.dot(slot_rows, up_slab, preferred_element_type=jnp.float32)
    sigmoid_gate = jax.nn.sigmoid(gate_pre)
    active = gate_pre * sigmoid_gate
    hidden = (active * up_pre).astype(jnp.bfloat16)
    partial_out = jnp.dot(hidden, down_slab, preferred_element_type=jnp.float32).astype(jnp.bfloat16)
    outer = (((1,), (1,)), ((), ()))
    inner = (((0,), (0,)), ((), ()))
    hidden_grad = lax.dot_general(scaled, down_slab, outer, preferred_element_type=jnp.float32)
    gate_pre_grad = (hidden_grad * up_pre * sigmoid_gate * (1.0 + gate_pre * (1.0 - sigmoid_gate))).astype(jnp.bfloat16)
    up_pre_grad = (hidden_grad * active).astype(jnp.bfloat16)
    grad_down = lax.dot_general(hidden, scaled, inner, preferred_element_type=jnp.float32).astype(jnp.bfloat16)
    grad_gate = lax.dot_general(slot_rows, gate_pre_grad, inner, preferred_element_type=jnp.float32).astype(jnp.bfloat16)
    grad_up = lax.dot_general(slot_rows, up_pre_grad, inner, preferred_element_type=jnp.float32).astype(jnp.bfloat16)
    back_rows = (lax.dot_general(gate_pre_grad, gate_slab, outer, preferred_element_type=jnp.float32)
                 + lax.dot_general(up_pre_grad, up_slab, outer, preferred_element_type=jnp.float32)).astype(jnp.bfloat16)
    return partial_out, back_rows, grad_gate, grad_up, grad_down


def reference(tokens, out_grad, experts, gate_values, slot_map, gate_weight, up_weight, down_weight):
    sources = N_GROUP * N_LOCAL
    expert_ids = jnp.arange(EXPERTS, dtype=jnp.int32)
    matched = experts[:, :, None] == expert_ids[None, None, :]
    picked = jnp.sum(matched.astype(jnp.int32), axis=1)
    weights = jnp.sum(jnp.where(matched, gate_values[:, :, None], 0.0), axis=1)
    blocks = picked.reshape(sources, TOK_DEV, EXPERTS)
    earlier = (jnp.cumsum(blocks, axis=1) - blocks).reshape(TOKENS, EXPERTS)
    group_base = jnp.arange(N_GROUP, dtype=jnp.int32)[:, None] * EPG
    owners = (slot_map // 2 + group_base).reshape(sources).astype(jnp.int32)
    rank_ids = jnp.arange(CAP, dtype=jnp.int32)
    positions = jnp.arange(TOKENS, dtype=jnp.int32).reshape(sources, TOK_DEV, 1)

    def one_device(carry, device):
        out_acc, back_acc, dots_acc = carry
        expert = owners[device]
        pick_col = picked[:, expert]
        rank_col = earlier[:, expert]
        weight_col = weights[:, expert]
        hits = ((pick_col[:, None] > 0) & (rank_col[:, None] == rank_ids[None, :])).reshape(sources, TOK_DEV, CAP)
        slot_index = jnp.sum(jnp.where(hits, positions, 0), axis=1).reshape(-1).astype(jnp.int32)
        filled = jnp.any(hits, axis=1).reshape(-1)
        slot_gate = jnp.sum(jnp.where(hits, weight_col.reshape(sources, TOK_DEV, 1), 0.0), axis=1).reshape(-1)
        slot_rows = jnp.where(filled[:, None], tokens[slot_index], jnp.zeros((), tokens.dtype))
        raw_grad = jnp.where(filled[:, None], out_grad[slot_index], jnp.zeros((), out_grad.dtype))
        scaled = (slot_gate[:, None] * raw_grad.astype(jnp.float32)).astype(jnp.bfloat16)
        partial_out, back_rows, grad_gate, grad_up, grad_down = expert_pass(
            slot_rows, scaled, gate_weight[device], up_weight[device], down_weight[device])
        partial_f = partial_out.astype(jnp.float32)
        slot_dots = jnp.sum(raw_grad.astype(jnp.float32) * partial_f, axis=1)
        out_acc = out_acc.at[slot_index].add(slot_gate[:, None] * partial_f)
        back_acc = back_acc.at[slot_index].add(back_rows.astype(jnp.float32))
        dots_acc = dots_acc.at[slot_index, expert].add(slot_dots)
        return (out_acc, back_acc, dots_acc), (grad_gate, grad_up, grad_down)

    start = (jnp.zeros((TOKENS, D), jnp.float32), jnp.zeros((TOKENS, D), jnp.float32),
             jnp.zeros((TOKENS, EXPERTS), jnp.float32))
    carry, grads = lax.scan(one_device, start, jnp.arange(sources, dtype=jnp.int32))
    out_acc, back_acc, dots_acc = carry
    gate_grad = jnp.sum(jnp.where(matched, dots_acc[:, None, :], 0.0), axis=2)
    return (out_acc.astype(jnp.bfloat16), back_acc.astype(jnp.bfloat16), gate_grad,
            grads[0], grads[1], grads[2])
```

```python
import jax
import jax.numpy as jnp
from jax import lax
from jax.sharding import Mesh
from jax.sharding import PartitionSpec as P

BF = jnp.bfloat16
F32 = jnp.float32
PLANE = ("y", "core", "x")
OFFSETS = (0, -1, 1, -2, 2, -3, 3, 4)
EXTRA = 128


def expert_pass(slot_rows, scaled, gate_slab, up_slab, down_slab):
    outer = (((1,), (1,)), ((), ()))
    inner = (((0,), (0,)), ((), ()))
    gate_pre = jnp.dot(slot_rows, gate_slab, preferred_element_type=F32)
    up_pre = jnp.dot(slot_rows, up_slab, preferred_element_type=F32)
    sigmoid_gate = jax.nn.sigmoid(gate_pre)
    active = gate_pre * sigmoid_gate
    hidden = (active * up_pre).astype(BF)
    partial_out = jnp.dot(hidden, down_slab, preferred_element_type=F32).astype(BF)
    hidden_grad = lax.dot_general(scaled, down_slab, outer, preferred_element_type=F32)
    gate_pre_grad = (
        hidden_grad * up_pre * sigmoid_gate * (1.0 + gate_pre * (1.0 - sigmoid_gate))
    ).astype(BF)
    up_pre_grad = (hidden_grad * active).astype(BF)
    back_rows = (
        lax.dot_general(gate_pre_grad, gate_slab, outer, preferred_element_type=F32)
        + lax.dot_general(up_pre_grad, up_slab, outer, preferred_element_type=F32)
    ).astype(BF)
    grad_down = lax.dot_general(hidden, scaled, inner, preferred_element_type=F32).astype(BF)
    grad_gate = lax.dot_general(slot_rows, gate_pre_grad, inner, preferred_element_type=F32).astype(BF)
    grad_up = lax.dot_general(slot_rows, up_pre_grad, inner, preferred_element_type=F32).astype(BF)
    return (partial_out, back_rows, grad_gate, grad_up, grad_down)


def shift(rows, step):
    n = lax.axis_size("z")
    return lax.ppermute(rows, "z", [(i, (i + step) % n) for i in range(n)])


def split_high(value):
    return lax.reduce_precision(value, 8, 7)


def ring_gather(rows):
    half = rows.shape[1] // 2 // 128 * 128
    ahead, behind, blocks = rows, rows, {0: rows}
    for k in range(1, 4):
        ahead, behind = shift(ahead, 1), shift(behind, -1)
        blocks[-k], blocks[k] = ahead, behind
    blocks[4] = jnp.concatenate([shift(ahead[:, :half], 1), shift(behind[:, half:], -1)], axis=1)
    return jnp.concatenate([blocks[k] for k in OFFSETS], axis=0)


def pack_sum(wide, dots):
    high = split_high(dots)
    low = dots - high
    pad = jnp.zeros((wide.shape[0], EXTRA - 2 * dots.shape[1]), BF)
    return jnp.concatenate([wide.astype(BF), high.astype(BF), low.astype(BF), pad], axis=1)


def unpack_sum(rows, top):
    rows = rows.astype(F32)
    wide = rows.shape[1] - EXTRA
    return rows[:, :wide], rows[:, wide : wide + top] + rows[:, wide + top : wide + 2 * top]


def ring_sum(wide, dots, here):
    top = dots.shape[1]
    half = wide.shape[1] // 2

    def block(k):
        at = OFFSETS.index(k) * here
        return wide[at : at + here], dots[at : at + here]

    far, far_dots = block(4)
    first = shift(far[:, :half].astype(BF), 1).astype(F32)
    second, second_dots = unpack_sum(shift(pack_sum(far[:, half:], far_dots), -1), top)
    ahead, ahead_dots = block(3)
    ahead = jnp.concatenate([ahead[:, :half] + first, ahead[:, half:]], axis=1)
    behind, behind_dots = block(-3)
    behind = jnp.concatenate([behind[:, :half], behind[:, half:] + second], axis=1)
    behind_dots = behind_dots + second_dots
    for k in (2, 1, 0):
        ahead, ahead_dots = unpack_sum(shift(pack_sum(ahead, ahead_dots), 1), top)
        behind, behind_dots = unpack_sum(shift(pack_sum(behind, behind_dots), -1), top)
        if k:
            own, own_dots = block(k)
            ahead, ahead_dots = ahead + own, ahead_dots + own_dots
            own, own_dots = block(-k)
            behind, behind_dots = behind + own, behind_dots + own_dots
    own, own_dots = block(0)
    return own + ahead + behind, own_dots + ahead_dots + behind_dots


def body(tokens, out_grad, experts, gate_values, slot_map, gate_weight, up_weight, down_weight):
    here, width = tokens.shape
    top = experts.shape[1]
    groups, members = slot_map.shape
    deep = lax.axis_size("z")
    across = lax.axis_size("x")
    per_group = members // 2
    capacity = 2 * here * top // (groups * per_group)
    dests = groups * across
    slots = deep * capacity
    held = deep * here

    gate_high = split_high(gate_values)
    gate_mid = split_high(gate_values - gate_high)
    gate_low = gate_values - gate_high - gate_mid
    extra = jnp.concatenate(
        [experts.astype(BF), gate_high.astype(BF), gate_mid.astype(BF), gate_low.astype(BF)]
        + [jnp.zeros((here, EXTRA - 4 * top), BF)],
        axis=1,
    )
    gathered = ring_gather(jnp.concatenate([tokens, out_grad, extra], axis=1))
    tok_all = gathered[:, :width]
    grad_all = gathered[:, width : 2 * width]
    info = gathered[:, 2 * width :].astype(F32)
    ids = info[:, :top].astype(jnp.int32)
    gates = info[:, top : 2 * top] + info[:, 2 * top : 3 * top] + info[:, 3 * top : 4 * top]

    column = lax.dynamic_slice_in_dim(slot_map, lax.axis_index("z") * across, across, axis=1)
    dest_expert = (column // 2 + jnp.arange(groups, dtype=jnp.int32)[:, None] * per_group).reshape(dests)
    matched = ids[:, :, None] == dest_expert[None, None, :]
    names = jnp.sum(matched.astype(F32), axis=1)
    weight = jnp.sum(jnp.where(matched, gates[:, :, None], 0.0), axis=1)
    rows_at = lax.broadcasted_iota(jnp.int32, (held, held), 0)
    cols_at = lax.broadcasted_iota(jnp.int32, (held, held), 1)
    before = ((rows_at // here == cols_at // here) & (cols_at < rows_at)).astype(BF)
    rank = jnp.dot(before, names.astype(BF), preferred_element_type=F32)
    code = jnp.where(names > 0.0, rank, -1.0).astype(jnp.int32).T
    weight_t = weight.T
    slot_shape = (dests, deep, capacity, held)
    block_at = lax.broadcasted_iota(jnp.int32, slot_shape, 1)
    rank_at = lax.broadcasted_iota(jnp.int32, slot_shape, 2)
    token_at = lax.broadcasted_iota(jnp.int32, slot_shape, 3)
    chosen = (code[:, None, None, :] == rank_at) & (token_at // here == block_at)
    chosen = chosen.reshape(dests * slots, held)
    mask = chosen.astype(BF)
    slot_weight = jnp.where(
        chosen.reshape(slot_shape), weight_t[:, None, None, :], 0.0
    ).reshape(dests * slots, held)

    slot_rows = jnp.dot(mask, tok_all, preferred_element_type=F32).astype(BF)
    raw_grad = jnp.dot(mask, grad_all, preferred_element_type=F32)
    scaled = (jnp.sum(slot_weight, axis=1)[:, None] * raw_grad).astype(BF)

    def exchange(rows):
        moved = lax.all_to_all(
            rows.reshape(dests, slots, width), PLANE, split_axis=0, concat_axis=0, tiled=True
        )
        return moved.reshape(dests * slots, width)

    arrived, arrived_grad = exchange(slot_rows), exchange(scaled)
    partial_out, back_rows, grad_gate, grad_up, grad_down = expert_pass(
        arrived, arrived_grad, gate_weight[0], up_weight[0], down_weight[0]
    )
    partial_back, back_back = exchange(partial_out), exchange(back_rows)

    inner = (((0,), (0,)), ((), ()))
    outer = (((1,), (1,)), ((), ()))
    weight_high = split_high(slot_weight)
    weight_low = (slot_weight - weight_high).astype(BF)
    layer_sum = lax.dot_general(
        weight_high.astype(BF), partial_back, inner, preferred_element_type=F32
    ) + lax.dot_general(weight_low, partial_back, inner, preferred_element_type=F32)
    token_sum = lax.dot_general(mask, back_back, inner, preferred_element_type=F32)
    dots = lax.dot_general(partial_back, grad_all, outer, preferred_element_type=F32)
    dots = jnp.sum(jnp.where(chosen, dots, 0.0).reshape(dests, slots, held), axis=1)
    gate_part = jnp.sum(jnp.where(matched, dots.T[:, None, :], 0.0), axis=2)

    wide, gate_grad = ring_sum(jnp.concatenate([layer_sum, token_sum], axis=1), gate_part, here)
    layer_out = wide[:, :width].astype(BF)
    token_grad = wide[:, width:].astype(BF)
    return (layer_out, token_grad, gate_grad, grad_gate[None], grad_up[None], grad_down[None])


def solution(mesh):
    groups, members = mesh.devices.shape
    fine = Mesh(
        mesh.devices.reshape(groups // 2, 2, members // 4, 4), ("y", "core", "z", "x")
    )
    every = ("y", "core", "z", "x")
    two, three = P(every, None), P(every, None, None)
    return jax.shard_map(
        body,
        mesh=fine,
        in_specs=(two, two, two, two, P(), three, three, three),
        out_specs=(two, two, two, three, three, three),
        check_vma=False,
    )
```

```python
import functools

import jax
import jax.numpy as jnp
from jax import lax
from jax.experimental import pallas as pl
from jax.experimental.pallas import tpu as pltpu
from jax.sharding import Mesh
from jax.sharding import PartitionSpec as P

BF = jnp.bfloat16
F32 = jnp.float32
PLANE = ("y", "core", "x")
OFFSETS = (0, -1, 1, -2, 2, -3, 3, 4)
EXTRA = 128
INNER = (((0,), (0,)), ((), ()))
OUTER = (((1,), (1,)), ((), ()))
VMEM_LIMIT = 56 * 1024 * 1024


def iota(shape, dim):
    return lax.broadcasted_iota(jnp.int32, shape, dim)


def identity(n):
    return (iota((n, n), 0) == iota((n, n), 1)).astype(BF)


def shift(rows, step):
    n = lax.axis_size("z")
    return lax.ppermute(rows, "z", [(i, (i + step) % n) for i in range(n)])


def ring_gather(rows, half):
    ahead, behind, blocks = rows, rows, {0: rows}
    for k in range(1, 4):
        ahead, behind = shift(ahead, 1), shift(behind, -1)
        blocks[-k], blocks[k] = ahead, behind
    blocks[4] = jnp.concatenate([shift(ahead[:, :half], 1), shift(behind[:, half:], -1)], axis=1)
    return jnp.concatenate([blocks[k] for k in OFFSETS], axis=0)


def ring_sum(rows, here, half):
    def block(k):
        at = OFFSETS.index(k) * here
        return rows[at : at + here]

    far = block(4).astype(BF)
    first = shift(far[:, :half], 1).astype(F32)
    second = shift(far[:, half:], -1).astype(F32)
    ahead, behind = block(3), block(-3)
    ahead = jnp.concatenate([ahead[:, :half] + first, ahead[:, half:]], axis=1).astype(BF)
    behind = jnp.concatenate([behind[:, :half], behind[:, half:] + second], axis=1).astype(BF)
    for k in (2, 1):
        ahead = (shift(ahead, 1).astype(F32) + block(k)).astype(BF)
        behind = (shift(behind, -1).astype(F32) + block(-k)).astype(BF)
    return block(0) + shift(ahead, 1).astype(F32) + shift(behind, -1).astype(F32)


def pick_slots(code, dests, slots, held):
    return code[:, None, :] == iota((dests, slots, held), 1).astype(F32)


def dispatch_kernel(here, top, dests, slots, rows_ref, expert_ref, out_ref, code_ref, weight_ref, ids_ref):
    held, wide = rows_ref.shape[0], out_ref.shape[1]
    width = wide // 2
    step = pl.program_id(0)
    deep = held // here

    @pl.when(step == 0)
    def _():
        info = rows_ref[:, wide:]
        info_t = lax.dot_general(identity(EXTRA), info, OUTER, preferred_element_type=F32)
        ids = info_t[:top]
        gates = info_t[top : 2 * top] + info_t[2 * top : 3 * top] + info_t[3 * top : 4 * top]
        dest_expert = expert_ref[...][:, :1]
        names = jnp.zeros((dests, held), F32)
        weight = jnp.zeros((dests, held), F32)
        for j in range(top):
            matched = ids[j : j + 1] == dest_expert
            names += jnp.where(matched, 1.0, 0.0)
            weight += jnp.where(matched, gates[j : j + 1], 0.0)
        first, later = iota((held, held), 0), iota((held, held), 1)
        before = ((first // here == later // here) & (first < later)).astype(BF)
        rank = jnp.dot(names.astype(BF), before, preferred_element_type=F32)
        block = (iota((dests, held), 1) // here).astype(F32)
        code_ref[...] = jnp.where(names > 0.0, rank * float(deep) + block, -1.0)
        weight_ref[...] = weight
        ids_ref[...] = ids

    part = out_ref.shape[0] // slots
    at = pl.ds(pl.multiple_of(step * part, part), part)
    chosen = pick_slots(code_ref[at, :], part, slots, held)
    mask = jnp.where(chosen, 1.0, 0.0).reshape(part * slots, held)
    weighted = jnp.where(chosen, weight_ref[at, :][:, None, :], 0.0).reshape(part * slots, held)
    slot_weight = jnp.sum(weighted, axis=1, keepdims=True)
    mask = mask.astype(BF)
    out_ref[:, :width] = jnp.dot(mask, rows_ref[:, :width], preferred_element_type=F32).astype(BF)
    raw = jnp.dot(mask, rows_ref[:, width:wide], preferred_element_type=F32)
    out_ref[:, width:] = (slot_weight * raw).astype(BF)


def dispatch(rows, dest_expert, here, top, slots, wide, steps=4):
    held = rows.shape[0]
    dests = dest_expert.shape[0]
    part = dests // steps
    whole = lambda shape: pl.BlockSpec(shape, lambda i: (0, 0))
    return pl.pallas_call(
        functools.partial(dispatch_kernel, here, top, dests, slots),
        grid=(steps,),
        in_specs=[whole(rows.shape), whole(dest_expert.shape)],
        out_specs=[
            pl.BlockSpec((part * slots, wide), lambda i: (i, 0)),
            whole((dests, held)),
            whole((dests, held)),
            whole((top, held)),
        ],
        out_shape=[
            jax.ShapeDtypeStruct((dests * slots, wide), BF),
            jax.ShapeDtypeStruct((dests, held), F32),
            jax.ShapeDtypeStruct((dests, held), F32),
            jax.ShapeDtypeStruct((top, held), F32),
        ],
        compiler_params=pltpu.CompilerParams(vmem_limit_bytes=VMEM_LIMIT),
        cost_estimate=pl.CostEstimate(
            flops=2 * dests * slots * held * wide, bytes_accessed=2 * dests * slots * wide, transcendentals=0
        ),
        name="dispatch",
    )(rows, dest_expert)


def expert_kernel(rows_ref, gate_ref, up_ref, down_ref, out_ref, hidden_ref, gate_grad_ref, up_grad_ref):
    width = gate_ref.shape[0]
    slot_rows = rows_ref[:, :width]
    scaled = rows_ref[:, width:]
    gate_pre = jnp.dot(slot_rows, gate_ref[...], preferred_element_type=F32)
    up_pre = jnp.dot(slot_rows, up_ref[...], preferred_element_type=F32)
    hidden_grad = lax.dot_general(scaled, down_ref[...], OUTER, preferred_element_type=F32)
    sigmoid_gate = jax.nn.sigmoid(gate_pre)
    active = gate_pre * sigmoid_gate
    hidden = (active * up_pre).astype(BF)
    gate_pre_grad = (
        hidden_grad * up_pre * sigmoid_gate * (1.0 + gate_pre * (1.0 - sigmoid_gate))
    ).astype(BF)
    up_pre_grad = (hidden_grad * active).astype(BF)
    hidden_ref[...] = hidden
    gate_grad_ref[...] = gate_pre_grad
    up_grad_ref[...] = up_pre_grad
    out_ref[:, :width] = jnp.dot(hidden, down_ref[...], preferred_element_type=F32).astype(BF)
    out_ref[:, width:] = (
        lax.dot_general(gate_pre_grad, gate_ref[...], OUTER, preferred_element_type=F32)
        + lax.dot_general(up_pre_grad, up_ref[...], OUTER, preferred_element_type=F32)
    ).astype(BF)


def run_expert(rows, gate_slab, up_slab, down_slab, steps=3):
    count, wide = rows.shape
    units = gate_slab.shape[1]
    part = count // steps
    whole = lambda a: pl.BlockSpec(a.shape, lambda i: (0, 0))
    chunk = lambda columns: pl.BlockSpec((part, columns), lambda i: (i, 0))
    return pl.pallas_call(
        expert_kernel,
        grid=(steps,),
        in_specs=[chunk(wide), whole(gate_slab), whole(up_slab), whole(down_slab)],
        out_specs=[chunk(wide), chunk(units), chunk(units), chunk(units)],
        out_shape=[jax.ShapeDtypeStruct((count, wide), BF)]
        + [jax.ShapeDtypeStruct((count, units), BF)] * 3,
        compiler_params=pltpu.CompilerParams(vmem_limit_bytes=VMEM_LIMIT),
        cost_estimate=pl.CostEstimate(
            flops=6 * count * units * wide,
            bytes_accessed=4 * count * wide + 3 * units * wide,
            transcendentals=count * units,
        ),
        name="expert",
    )(rows, gate_slab, up_slab, down_slab)


def combine_kernel(slots, back_ref, grad_ref, code_ref, weight_ref, ids_ref, expert_ref, out_ref, dots_ref):
    held, width = grad_ref.shape
    step = pl.program_id(0)
    part = back_ref.shape[0] // slots
    at = pl.ds(pl.multiple_of(step * part, part), part)

    @pl.when(step == 0)
    def _():
        out_ref[...] = jnp.zeros_like(out_ref)

    chosen = pick_slots(code_ref[at, :], part, slots, held)
    weighted = jnp.where(chosen, weight_ref[at, :][:, None, :], 0.0).reshape(part * slots, held)
    high = weighted.astype(BF)
    low = (weighted - high.astype(F32)).astype(BF)
    mask = jnp.where(chosen, 1.0, 0.0).reshape(part * slots, held).astype(BF)
    partial_rows = back_ref[:, :width]
    out_ref[:, :width] += lax.dot_general(
        high, partial_rows, INNER, preferred_element_type=F32
    ) + lax.dot_general(low, partial_rows, INNER, preferred_element_type=F32)
    out_ref[:, width : 2 * width] += lax.dot_general(
        mask, back_ref[:, width:], INNER, preferred_element_type=F32
    )
    dots = lax.dot_general(partial_rows, grad_ref[...], OUTER, preferred_element_type=F32)
    dots = jnp.where(chosen, dots.reshape(part, slots, held), 0.0)
    dots_ref[at, :] = jnp.sum(dots, axis=1)

    @pl.when(step == pl.num_programs(0) - 1)
    def _():
        dest_expert = expert_ref[...][:, :1]
        rows = [
            jnp.sum(jnp.where(ids_ref[j : j + 1, :] == dest_expert, dots_ref[...], 0.0), axis=0, keepdims=True)
            for j in range(ids_ref.shape[0])
        ]
        gate = jnp.concatenate(rows + [jnp.zeros((EXTRA - len(rows), held), F32)], axis=0)
        high = gate.astype(BF)
        low = (gate - high.astype(F32)).astype(BF)
        out_ref[:, 2 * width :] = lax.dot_general(
            high, identity(EXTRA), INNER, preferred_element_type=F32
        ) + lax.dot_general(low, identity(EXTRA), INNER, preferred_element_type=F32)


def combine(returned, rows, code, weight, ids, dest_expert, slots, steps=4):
    count, wide = returned.shape
    held = rows.shape[0]
    dests = code.shape[0]
    width = wide // 2
    whole = lambda a: pl.BlockSpec(a.shape, lambda i: (0, 0))
    return pl.pallas_call(
        functools.partial(combine_kernel, slots),
        grid=(steps,),
        in_specs=[
            pl.BlockSpec((count // steps, wide), lambda i: (i, 0)),
            pl.BlockSpec((held, width), lambda i: (0, 1)),
            whole(code),
            whole(weight),
            whole(ids),
            whole(dest_expert),
        ],
        out_specs=pl.BlockSpec((held, wide + EXTRA), lambda i: (0, 0)),
        out_shape=jax.ShapeDtypeStruct((held, wide + EXTRA), F32),
        scratch_shapes=[pltpu.VMEM((dests, held), F32)],
        compiler_params=pltpu.CompilerParams(vmem_limit_bytes=VMEM_LIMIT),
        cost_estimate=pl.CostEstimate(
            flops=4 * count * held * wide, bytes_accessed=2 * count * wide, transcendentals=0
        ),
        name="combine",
    )(returned, rows, code, weight, ids, dest_expert)


def split_high(value):
    return lax.reduce_precision(value, 8, 7)


def body(tokens, out_grad, experts, gate_values, slot_map, gate_weight, up_weight, down_weight):
    here, width = tokens.shape
    top = experts.shape[1]
    groups, members = slot_map.shape
    deep = lax.axis_size("z")
    across = lax.axis_size("x")
    per_group = members // 2
    capacity = 2 * here * top // (groups * per_group)
    dests = groups * across
    slots = deep * capacity
    wide = 2 * width

    gate_high = split_high(gate_values)
    gate_mid = split_high(gate_values - gate_high)
    gate_low = gate_values - gate_high - gate_mid
    extra = jnp.concatenate([experts.astype(F32), gate_high, gate_mid, gate_low], axis=1)
    extra = jnp.pad(extra, ((0, 0), (0, EXTRA - 4 * top))).astype(BF)
    rows = ring_gather(jnp.concatenate([tokens, out_grad, extra], axis=1), width)

    column = lax.dynamic_slice_in_dim(slot_map, lax.axis_index("z") * across, across, axis=1)
    dest_expert = column // 2 + jnp.arange(groups, dtype=jnp.int32)[:, None] * per_group
    dest_expert = jnp.broadcast_to(dest_expert.reshape(dests, 1).astype(F32), (dests, 128))

    def exchange(rows):
        moved = lax.all_to_all(
            rows.reshape(dests, slots, wide), PLANE, split_axis=0, concat_axis=0, tiled=True
        )
        return moved.reshape(dests * slots, wide)

    sent, code, weight, ids = dispatch(rows, dest_expert, here, top, slots, wide)
    arrived = exchange(sent)
    results, hidden, gate_pre_grad, up_pre_grad = run_expert(
        arrived, gate_weight[0], up_weight[0], down_weight[0]
    )
    returned = exchange(results)
    slot_rows, scaled = arrived[:, :width], arrived[:, width:]
    grad_down = lax.dot_general(hidden, scaled, INNER, preferred_element_type=F32).astype(BF)
    grad_gate = lax.dot_general(slot_rows, gate_pre_grad, INNER, preferred_element_type=F32).astype(BF)
    grad_up = lax.dot_general(slot_rows, up_pre_grad, INNER, preferred_element_type=F32).astype(BF)

    sums = combine(returned, rows, code, weight, ids, dest_expert, slots)
    total = ring_sum(sums, here, width)
    layer_out = total[:, :width].astype(BF)
    token_grad = total[:, width:wide].astype(BF)
    gate_grad = total[:, wide : wide + top]
    return (layer_out, token_grad, gate_grad, grad_gate[None], grad_up[None], grad_down[None])


def solution(mesh):
    groups, members = mesh.devices.shape
    fine = Mesh(
        mesh.devices.reshape(groups // 2, 2, members // 4, 4), ("y", "core", "z", "x")
    )
    every = ("y", "core", "z", "x")
    two, three = P(every, None), P(every, None, None)
    return jax.shard_map(
        body,
        mesh=fine,
        in_specs=(two, two, two, two, P(), three, three, three),
        out_specs=(two, two, two, three, three, three),
        check_vma=False,
    )
```

```python
import functools

import jax
import jax.numpy as jnp
from jax import lax
from jax.experimental import pallas as pl
from jax.experimental.pallas import tpu as pltpu
from jax.sharding import Mesh
from jax.sharding import PartitionSpec as P

BF = jnp.bfloat16
F32 = jnp.float32
SPREAD = ("y", "core", "zlo", "x")
EXTRA = 128
SORT = 8
STEPS = (0, 1, 2, 3)
INNER = (((0,), (0,)), ((), ()))
OUTER = (((1,), (1,)), ((), ()))
VMEM_LIMIT = 48 * 1024 * 1024


def iota(shape, dim):
    return lax.broadcasted_iota(jnp.int32, shape, dim)


def identity(n):
    return (iota((n, n), 0) == iota((n, n), 1)).astype(BF)


def whole(a):
    return pl.BlockSpec(a.shape, lambda i: (0, 0))


def cost(flops, moved, special=0):
    return pl.CostEstimate(flops=flops, bytes_accessed=moved, transcendentals=special)


def params():
    return pltpu.CompilerParams(vmem_limit_bytes=VMEM_LIMIT)


def make_tables(here, top, slots, info, dest_expert, code_ref, weight_ref, ids_ref):
    dests, held = code_ref.shape
    info_t = lax.dot_general(identity(EXTRA), info, OUTER, preferred_element_type=F32)
    ids = info_t[:top]
    gates = info_t[top : 2 * top] + info_t[2 * top : 3 * top] + info_t[3 * top : 4 * top]
    names = jnp.zeros((dests, held), F32)
    weight = jnp.zeros((dests, held), F32)
    for j in range(top):
        matched = ids[j : j + 1] == dest_expert
        names += jnp.where(matched, 1.0, 0.0)
        weight += jnp.where(matched, gates[j : j + 1], 0.0)
    first, later = iota((held, held), 0), iota((held, held), 1)
    before = ((first // here == later // here) & (first < later)).astype(BF)
    rank = jnp.dot(names.astype(BF), before, preferred_element_type=F32)
    row = iota((dests, held), 1)
    blocks = held // (2 * here)
    place = row // (2 * here) + row // here % 2 * (slots // 2)
    code_ref[...] = jnp.where(names > 0.0, rank * float(blocks) + place.astype(F32), -1.0)
    weight_ref[...] = weight
    ids_ref[...] = ids


def pack_kernel(tokens_ref, out_grad_ref, experts_ref, gates_ref, out_ref):
    here, width = tokens_ref.shape
    top = experts_ref.shape[0]
    gates = gates_ref[...]
    high = gates.astype(BF)
    middle = (gates - high.astype(F32)).astype(BF)
    low = (gates - high.astype(F32) - middle.astype(F32)).astype(BF)
    extra = jnp.zeros((here, EXTRA), F32)
    for k, part in enumerate((experts_ref[...].astype(F32).astype(BF), high, middle, low)):
        place = (iota((top, EXTRA), 0) + k * top == iota((top, EXTRA), 1)).astype(BF)
        extra += lax.dot_general(part, place, INNER, preferred_element_type=F32)
    rows = [tokens_ref[...].astype(F32), out_grad_ref[...].astype(F32)]
    out_ref[:, :width] = jnp.concatenate(rows, axis=0).astype(BF)
    out_ref[:, width:] = jnp.concatenate([extra, extra], axis=0).astype(BF)


def pack(tokens, out_grad, experts_t, gates_t):
    here, width = tokens.shape
    return pl.pallas_call(
        pack_kernel,
        out_shape=jax.ShapeDtypeStruct((2 * here, width + EXTRA), BF),
        name="pack",
    )(tokens, out_grad, experts_t, gates_t)


def fill_kernel(here, top, slots, rows_ref, expert_ref, out_ref, code_ref, weight_ref, ids_ref):
    held, width = rows_ref.shape[0], out_ref.shape[1]
    step = pl.program_id(0)

    @pl.when(step == 0)
    def _():
        make_tables(here, top, slots, rows_ref[:, width:], expert_ref[...][:, :1], code_ref, weight_ref, ids_ref)

    part = out_ref.shape[0] // slots
    at = pl.ds(pl.multiple_of(step * part, part), part)
    chosen = code_ref[at, :][:, None, :] == iota((part, slots, held), 1).astype(F32)
    scale = jnp.where(iota((part, held), 1) // here % 2 == 0, 1.0, weight_ref[at, :])
    scaled = jnp.where(chosen, scale[:, None, :], 0.0).reshape(part * slots, held)
    scale = jnp.sum(scaled, axis=1, keepdims=True)
    mask = jnp.where(chosen, 1.0, 0.0).reshape(part * slots, held).astype(BF)
    raw = jnp.dot(mask, rows_ref[:, :width], preferred_element_type=F32)
    out_ref[...] = (scale * raw).astype(BF)


def fill(rows, dest_expert, here, top, slots, width, steps=4):
    held = rows.shape[0]
    dests = dest_expert.shape[0]
    part = dests // steps * slots
    tables = [(dests, held), (dests, held), (top, held)]
    return pl.pallas_call(
        functools.partial(fill_kernel, here, top, slots),
        grid=(steps,),
        in_specs=[whole(rows), whole(dest_expert)],
        out_specs=[pl.BlockSpec((part, width), lambda i: (i, 0))]
        + [pl.BlockSpec(shape, lambda i: (0, 0)) for shape in tables],
        out_shape=[jax.ShapeDtypeStruct((dests * slots, width), BF)]
        + [jax.ShapeDtypeStruct(shape, F32) for shape in tables],
        compiler_params=params(),
        cost_estimate=cost(2 * dests * slots * held * width, 2 * dests * slots * width),
        name="fill",
    )(rows, dest_expert)


def sorting(slots, transposed=False):
    half, count = slots // 2, SORT * slots
    a, b = iota((count, count), 0), iota((count, count), 1)
    if transposed:
        a, b = b, a
    kind, place = a // (SORT * half), a % (SORT * half)
    return (place // half * slots + kind * half + place % half == b).astype(BF)


def sort_rows(order, rows):
    return jnp.dot(order, rows, preferred_element_type=F32).astype(BF)


def kind_rows(kind, slots, rows_ref):
    count = SORT * slots
    half = count // 2
    place, at = iota((half, count), 0), iota((half, count), 1)
    order = (place // (slots // 2) * slots + kind * (slots // 2) + place % (slots // 2) == at).astype(BF)
    parts = [sort_rows(order, rows_ref[i : i + count, :]) for i in range(0, rows_ref.shape[0], count)]
    return jnp.concatenate(parts, axis=0)


def split_rows(slots, rows, out_ref):
    order = sorting(slots, transposed=True)
    count = order.shape[0]
    half, features = count // 2, rows.shape[1] // 2
    for i in range(rows.shape[0] // half):
        part = rows[i * half : (i + 1) * half]
        both = jnp.concatenate([part[:, :features], part[:, features:]], axis=0)
        out_ref[i * count : (i + 1) * count, :] = sort_rows(order, both)


def forward_kernel(slots, rows_ref, gate_ref, up_ref, down_ref, out_ref, hidden_ref, active_ref, slope_ref):
    slot_rows = kind_rows(0, slots, rows_ref)
    gate_pre = jnp.dot(slot_rows, gate_ref[...], preferred_element_type=F32)
    up_pre = jnp.dot(slot_rows, up_ref[...], preferred_element_type=F32)
    sigmoid_gate = jax.nn.sigmoid(gate_pre)
    active = gate_pre * sigmoid_gate
    hidden = (active * up_pre).astype(BF)
    hidden_ref[...] = hidden
    active_ref[...] = active
    slope_ref[...] = up_pre * sigmoid_gate * (1.0 + gate_pre * (1.0 - sigmoid_gate))
    partial_rows = jnp.dot(hidden, down_ref[...], preferred_element_type=F32).astype(BF)
    split_rows(slots, partial_rows, out_ref)


def backward_kernel(slots, rows_ref, active_ref, slope_ref, gate_ref, up_ref, down_ref,
                    out_ref, gate_grad_ref, up_grad_ref):
    scaled = kind_rows(1, slots, rows_ref)
    hidden_grad = lax.dot_general(scaled, down_ref[...], OUTER, preferred_element_type=F32)
    gate_pre_grad = (hidden_grad * slope_ref[...]).astype(BF)
    up_pre_grad = (hidden_grad * active_ref[...]).astype(BF)
    gate_grad_ref[...] = gate_pre_grad
    up_grad_ref[...] = up_pre_grad
    back_rows = (
        lax.dot_general(gate_pre_grad, gate_ref[...], OUTER, preferred_element_type=F32)
        + lax.dot_general(up_pre_grad, up_ref[...], OUTER, preferred_element_type=F32)
    ).astype(BF)
    split_rows(slots, back_rows, out_ref)


def expert_call(kernel, rows, kept, slabs, outs, name, slots, steps=4):
    count, width = rows.shape
    units = slabs[0].shape[1]
    chunk = lambda size, columns: pl.BlockSpec((size // steps, columns), lambda i: (i, 0))
    return pl.pallas_call(
        functools.partial(kernel, slots),
        grid=(steps,),
        in_specs=[chunk(count, width)] + [chunk(count // 2, units)] * len(kept) + [whole(a) for a in slabs],
        out_specs=[chunk(count, width // 2)] + [chunk(count // 2, units)] * len(outs),
        out_shape=[jax.ShapeDtypeStruct((count, width // 2), BF)]
        + [jax.ShapeDtypeStruct((count // 2, units), kind) for kind in outs],
        compiler_params=params(),
        cost_estimate=cost(3 * count * units * width, 3 * count * width + 6 * units * width, count * units),
        name=name,
    )(rows, *kept, *slabs)


def slab_grad_kernel(slots, rows_ref, hidden_ref, gate_grad_ref, up_grad_ref, gate_out, up_out, down_out, token_ref, grad_ref):
    count = SORT * slots
    half = count // 2
    order = sorting(slots)
    for i in range(rows_ref.shape[0] // count):
        rows = sort_rows(order, rows_ref[i * count : (i + 1) * count, :])
        token_ref[i * half : (i + 1) * half, :] = rows[:half]
        grad_ref[i * half : (i + 1) * half, :] = rows[half:]
    slot_rows = token_ref[...]
    gate_out[...] = lax.dot_general(slot_rows, gate_grad_ref[...], INNER, preferred_element_type=F32).astype(BF)
    up_out[...] = lax.dot_general(slot_rows, up_grad_ref[...], INNER, preferred_element_type=F32).astype(BF)
    down_out[...] = lax.dot_general(hidden_ref[...], grad_ref[...], INNER, preferred_element_type=F32).astype(BF)


def slab_grads(rows, hidden, gate_pre_grad, up_pre_grad, slots, steps=4):
    count, width = rows.shape
    units = hidden.shape[1]
    part = width // steps
    return pl.pallas_call(
        functools.partial(slab_grad_kernel, slots),
        grid=(steps,),
        in_specs=[pl.BlockSpec((count, part), lambda i: (0, i)), whole(hidden), whole(hidden), whole(hidden)],
        out_specs=[pl.BlockSpec((part, units), lambda i: (i, 0))] * 2
        + [pl.BlockSpec((units, part), lambda i: (0, i))],
        out_shape=[jax.ShapeDtypeStruct((width, units), BF)] * 2 + [jax.ShapeDtypeStruct((units, width), BF)],
        scratch_shapes=[pltpu.VMEM((count // 2, part), BF)] * 2,
        compiler_params=params(),
        cost_estimate=cost(3 * count * units * width, 2 * count * width + 6 * units * width),
        name="slab_grads",
    )(rows, hidden, gate_pre_grad, up_pre_grad)


def by_row(table, slots, count):
    repeat = (iota((table.shape[0], count), 1) // slots == iota((table.shape[0], count), 0)).astype(BF)
    return lax.dot_general(table.astype(BF), repeat, INNER, preferred_element_type=F32)


def prepare_kernel(here, slots, rows_ref, code_ref, weight_ref, high_ref, low_ref, mask_ref, grad_ref):
    held, count = high_ref.shape
    half = grad_ref.shape[1]
    slot = (iota((held, count), 1) % slots).astype(F32)
    chosen = by_row(code_ref[...], slots, count) == slot
    weight = weight_ref[...]
    high = weight.astype(BF).astype(F32)
    mask_ref[...] = jnp.where(chosen, 1.0, 0.0).astype(BF)
    high_ref[...] = jnp.where(chosen, by_row(high, slots, count), 0.0).astype(BF)
    low_ref[...] = jnp.where(chosen, by_row(weight - high, slots, count), 0.0).astype(BF)
    for k in range(0, held, 2 * here):
        rows = rows_ref[k : k + 2 * here, : 2 * half].astype(F32)[here:]
        grad_ref[k : k + 2 * here, :] = jnp.concatenate([rows[:, :half], rows[:, half:]], axis=0).astype(BF)


def prepare(rows, code, weight, here, slots):
    held, wide = rows.shape
    count = code.shape[0] * slots
    return pl.pallas_call(
        functools.partial(prepare_kernel, here, slots),
        out_shape=[jax.ShapeDtypeStruct((held, count), BF)] * 3
        + [jax.ShapeDtypeStruct((held, (wide - EXTRA) // 2), BF)],
        compiler_params=params(),
        name="prepare",
    )(rows, code, weight)


def store_blocks(index_ref, total_ref, outs, columns):
    size = outs[0].shape[0]
    for k, out_ref in zip(STEPS, outs):
        at = pl.multiple_of((index_ref[0, 0] + k) % len(outs) * size, size)
        out_ref[:, columns] = total_ref[pl.ds(at, size), :].astype(BF)


def layer_sum_kernel(slots, index_ref, back_ref, rows_ref, code_ref, ids_ref, expert_ref, high_ref, low_ref, *refs):
    *outs, total_ref, gate_ref, dots_ref = refs
    held = high_ref.shape[0]
    top = ids_ref.shape[0]
    dests = code_ref.shape[0]
    part = back_ref.shape[1]
    half = outs[0].shape[1] - EXTRA
    step = pl.program_id(0)

    @pl.when(step == 0)
    def _():
        dots_ref[...] = jnp.zeros_like(dots_ref)

    back = back_ref[...]
    total_ref[...] = jnp.dot(high_ref[...], back, preferred_element_type=F32) + jnp.dot(
        low_ref[...], back, preferred_element_type=F32
    )
    store_blocks(index_ref, total_ref, outs, pl.ds(pl.multiple_of(step * part, part), part))
    dots_ref[...] += lax.dot_general(back, rows_ref[...], OUTER, preferred_element_type=F32)

    @pl.when(step == pl.num_programs(0) - 1)
    def _():
        chosen = code_ref[...][:, None, :] == iota((dests, slots, held), 1).astype(F32)
        by_dest = jnp.sum(jnp.where(chosen, dots_ref[...].reshape(dests, slots, held), 0.0), axis=1)
        dest_expert = expert_ref[...][:, :1]
        rows = [
            jnp.sum(jnp.where(ids_ref[j : j + 1, :] == dest_expert, by_dest, 0.0), axis=0, keepdims=True)
            for j in range(top)
        ]
        gate = jnp.concatenate(rows + [jnp.zeros((EXTRA - top, held), F32)], axis=0)
        gate_ref[...] = lax.dot_general(gate.astype(BF), identity(EXTRA), INNER, preferred_element_type=F32)
        store_blocks(index_ref, gate_ref, outs, slice(half, half + EXTRA))


def layer_sums(index, returned, rows, code, ids, dest_expert, high, low, slots, steps=2):
    count, half = returned.shape
    held = rows.shape[0]
    size = held // len(STEPS)
    part = half // steps
    chunk = lambda size: pl.BlockSpec((size, part), lambda i: (0, i))
    return pl.pallas_call(
        functools.partial(layer_sum_kernel, slots),
        grid=(steps,),
        in_specs=[pl.BlockSpec(memory_space=pltpu.SMEM), chunk(count), chunk(held)]
        + [whole(a) for a in (code, ids, dest_expert, high, low)],
        out_specs=[pl.BlockSpec((size, half + EXTRA), lambda i: (0, 0))] * len(STEPS),
        out_shape=[jax.ShapeDtypeStruct((size, half + EXTRA), BF)] * len(STEPS),
        scratch_shapes=[
            pltpu.VMEM((held, part), F32),
            pltpu.VMEM((held, EXTRA), F32),
            pltpu.VMEM((count, held), F32),
        ],
        compiler_params=params(),
        cost_estimate=cost(6 * count * held * half, 2 * count * half),
        name="layer_sums",
    )(index, returned, rows, code, ids, dest_expert, high, low)


def token_sum_kernel(index_ref, back_ref, mask_ref, *refs):
    *outs, total_ref = refs
    total_ref[...] = jnp.dot(mask_ref[...], back_ref[...], preferred_element_type=F32)
    store_blocks(index_ref, total_ref, outs, slice(None))


def token_sums(index, returned, mask, steps=2):
    count, half = returned.shape
    held = mask.shape[0]
    size = held // len(STEPS)
    part = half // steps
    chunk = lambda size: pl.BlockSpec((size, part), lambda i: (0, i))
    return pl.pallas_call(
        token_sum_kernel,
        grid=(steps,),
        in_specs=[pl.BlockSpec(memory_space=pltpu.SMEM), chunk(count), whole(mask)],
        out_specs=[chunk(size)] * len(STEPS),
        out_shape=[jax.ShapeDtypeStruct((size, half), BF)] * len(STEPS),
        scratch_shapes=[pltpu.VMEM((held, part), F32)],
        compiler_params=params(),
        cost_estimate=cost(2 * count * held * half, 2 * count * half),
        name="token_sums",
    )(index, returned, mask)


def sum_blocks(sums):
    n = lax.axis_size("zhi")
    total = sums[0].astype(F32)
    for rows, step in zip(sums[1:], STEPS[1:]):
        moved = lax.ppermute(rows, "zhi", [(i, (i + step) % n) for i in range(n)])
        total += moved.astype(F32)
    return total


def body(tokens, out_grad, experts, gate_values, slot_map, gate_weight, up_weight, down_weight):
    here, width = tokens.shape
    top = experts.shape[1]
    groups, members = slot_map.shape
    blocks = len(STEPS)
    near = members // blocks
    per_group = members // 2
    capacity = 2 * here * top // (groups * per_group)
    dests = groups * near
    slots = 2 * blocks * capacity

    own = pack(tokens, out_grad, experts.T, gate_values.T)
    rows = lax.all_gather(own, "zhi", axis=0, tiled=True)

    column = lax.dynamic_slice_in_dim(slot_map, lax.axis_index("zhi") * near, near, axis=1)
    dest_expert = column // 2 + jnp.arange(groups, dtype=jnp.int32)[:, None] * per_group
    dest_expert = jnp.broadcast_to(dest_expert.reshape(dests, 1).astype(F32), (dests, 128))

    def exchange(rows):
        columns = rows.shape[1]
        moved = lax.all_to_all(
            rows.reshape(dests, slots, columns), SPREAD, split_axis=0, concat_axis=0, tiled=True
        )
        return moved.reshape(dests * slots, columns)

    after = lax.optimization_barrier
    index = lax.axis_index("zhi").astype(jnp.int32).reshape(1, 1)
    slabs = (gate_weight[0], up_weight[0], down_weight[0])
    sent, code, weight, ids = fill(rows, dest_expert, here, top, slots, width)
    arrived = exchange(sent)
    partial_out, hidden, active, slope = expert_call(
        forward_kernel, arrived, (), slabs, (BF, F32, F32), "forward", slots
    )
    partial_out, arrived, rows = after((partial_out, arrived, rows))
    partial_back = exchange(partial_out)
    back_rows, gate_pre_grad, up_pre_grad = expert_call(
        backward_kernel, arrived, (active, slope), slabs, (BF, BF), "backward", slots
    )
    grad_gate, grad_up, grad_down = slab_grads(arrived, hidden, gate_pre_grad, up_pre_grad, slots)
    high, low, mask, grads = prepare(rows, code, weight, here, slots)
    back_rows, partial_back, high, low, mask, grads, grad_gate, grad_up, grad_down = after(
        (back_rows, partial_back, high, low, mask, grads, grad_gate, grad_up, grad_down)
    )
    back_back = exchange(back_rows)
    layer = sum_blocks(layer_sums(index, partial_back, grads, code, ids, dest_expert, high, low, slots))
    back_back, layer = after((back_back, layer))
    token = sum_blocks(token_sums(index, back_back, mask))

    half = width // 2
    layer_out = jnp.concatenate([layer[:here, :half], layer[here:, :half]], axis=1).astype(BF)
    gate_grad = layer[:here, half : half + top] + layer[here:, half : half + top]
    token_grad = jnp.concatenate([token[:here], token[here:]], axis=1).astype(BF)
    return (layer_out, token_grad, gate_grad, grad_gate[None], grad_up[None], grad_down[None])


def solution(mesh):
    groups, members = mesh.devices.shape
    axes = ("y", "core", "zhi", "zlo", "x")
    fine = Mesh(mesh.devices.reshape(groups // 2, 2, members // 8, 2, 4), axes)
    two, three = P(axes, None), P(axes, None, None)
    return jax.shard_map(
        body,
        mesh=fine,
        in_specs=(two, two, two, two, P(), three, three, three),
        out_specs=(two, two, two, three, three, three),
        check_vma=False,
    )
```

```python
import functools

import jax
import jax.numpy as jnp
from jax import lax
from jax.experimental import pallas as pl
from jax.experimental.pallas import tpu as pltpu
from jax.sharding import Mesh
from jax.sharding import PartitionSpec as P

BF = jnp.bfloat16
F32 = jnp.float32
SPREAD = ("y", "core", "zlo", "x")
EXTRA = 128
STEPS = (0, 1, 2, 3)
INNER = (((0,), (0,)), ((), ()))
OUTER = (((1,), (1,)), ((), ()))
VMEM_LIMIT = 48 * 1024 * 1024


def iota(shape, dim):
    return lax.broadcasted_iota(jnp.int32, shape, dim)


def identity(n):
    return (iota((n, n), 0) == iota((n, n), 1)).astype(BF)


def whole(a):
    return pl.BlockSpec(a.shape, lambda i: (0, 0))


def cost(flops, moved, special=0):
    return pl.CostEstimate(flops=flops, bytes_accessed=moved, transcendentals=special)


def params():
    return pltpu.CompilerParams(vmem_limit_bytes=VMEM_LIMIT)


def make_tables(here, top, slots, info, dest_expert, code_ref, weight_ref, ids_ref):
    dests, held = code_ref.shape
    info_t = lax.dot_general(identity(EXTRA), info, OUTER, preferred_element_type=F32)
    ids = info_t[:top]
    gates = info_t[top : 2 * top] + info_t[2 * top : 3 * top] + info_t[3 * top : 4 * top]
    names = jnp.zeros((dests, held), F32)
    weight = jnp.zeros((dests, held), F32)
    for j in range(top):
        matched = ids[j : j + 1] == dest_expert
        names += jnp.where(matched, 1.0, 0.0)
        weight += jnp.where(matched, gates[j : j + 1], 0.0)
    first, later = iota((held, held), 0), iota((held, held), 1)
    before = ((first // here == later // here) & (first < later)).astype(BF)
    rank = jnp.dot(names.astype(BF), before, preferred_element_type=F32)
    row = iota((dests, held), 1)
    blocks = held // (2 * here)
    place = row // (2 * here) + row // here % 2 * (slots // 2)
    code_ref[...] = jnp.where(names > 0.0, rank * float(blocks) + place.astype(F32), -1.0)
    weight_ref[...] = weight
    ids_ref[...] = ids


def pack_kernel(tokens_ref, out_grad_ref, experts_ref, gates_ref, out_ref):
    here, width = tokens_ref.shape
    top = experts_ref.shape[0]
    gates = gates_ref[...]
    high = gates.astype(BF)
    middle = (gates - high.astype(F32)).astype(BF)
    low = (gates - high.astype(F32) - middle.astype(F32)).astype(BF)
    extra = jnp.zeros((here, EXTRA), F32)
    for k, part in enumerate((experts_ref[...].astype(F32).astype(BF), high, middle, low)):
        place = (iota((top, EXTRA), 0) + k * top == iota((top, EXTRA), 1)).astype(BF)
        extra += lax.dot_general(part, place, INNER, preferred_element_type=F32)
    rows = [tokens_ref[...].astype(F32), out_grad_ref[...].astype(F32)]
    out_ref[:, :width] = jnp.concatenate(rows, axis=0).astype(BF)
    out_ref[:, width:] = jnp.concatenate([extra, extra], axis=0).astype(BF)


def pack(tokens, out_grad, experts_t, gates_t):
    here, width = tokens.shape
    return pl.pallas_call(
        pack_kernel,
        out_shape=jax.ShapeDtypeStruct((2 * here, width + EXTRA), BF),
        name="pack",
    )(tokens, out_grad, experts_t, gates_t)


def dest_experts(index, slot_map, dests):
    groups, members = slot_map.shape
    near = dests // groups
    row = (iota((dests, groups), 0) // near == iota((dests, groups), 1)).astype(BF)
    held = jnp.dot(row, slot_map.astype(F32).astype(BF), preferred_element_type=F32)
    column = index * near + iota((dests, members), 0) % near
    held = jnp.sum(jnp.where(iota((dests, members), 1) == column, held, 0.0), axis=1, keepdims=True)
    first = iota((dests, 1), 0) // near * (members // 2)
    return (held.astype(jnp.int32) // 2 + first).astype(F32)


def fill_kernel(here, top, slots, index_ref, rows_ref, map_ref, out_ref, code_ref, weight_ref, ids_ref, expert_ref):
    held, width = rows_ref.shape[0], out_ref.shape[1]
    step = pl.program_id(0)

    @pl.when(step == 0)
    def _():
        dest_expert = dest_experts(index_ref[0, 0], map_ref[...], code_ref.shape[0])
        make_tables(here, top, slots, rows_ref[:, width:], dest_expert, code_ref, weight_ref, ids_ref)
        expert_ref[...] = jnp.broadcast_to(dest_expert, expert_ref.shape)

    part = out_ref.shape[0] // slots
    at = pl.ds(pl.multiple_of(step * part, part), part)
    chosen = code_ref[at, :][:, None, :] == iota((part, slots, held), 1).astype(F32)
    scale = jnp.where(iota((part, held), 1) // here % 2 == 0, 1.0, weight_ref[at, :])
    scaled = jnp.where(chosen, scale[:, None, :], 0.0).reshape(part * slots, held)
    scale = jnp.sum(scaled, axis=1, keepdims=True)
    mask = jnp.where(chosen, 1.0, 0.0).reshape(part * slots, held).astype(BF)
    raw = jnp.dot(mask, rows_ref[:, :width], preferred_element_type=F32)
    out_ref[...] = (scale * raw).astype(BF)


def fill(index, rows, slot_map, dests, here, top, slots, width, steps=4):
    held = rows.shape[0]
    part = dests // steps * slots
    tables = [(dests, held), (dests, held), (top, held), (dests, 128)]
    return pl.pallas_call(
        functools.partial(fill_kernel, here, top, slots),
        grid=(steps,),
        in_specs=[pl.BlockSpec(memory_space=pltpu.SMEM), whole(rows), whole(slot_map)],
        out_specs=[pl.BlockSpec((part, width), lambda i: (i, 0))]
        + [pl.BlockSpec(shape, lambda i: (0, 0)) for shape in tables],
        out_shape=[jax.ShapeDtypeStruct((dests * slots, width), BF)]
        + [jax.ShapeDtypeStruct(shape, F32) for shape in tables],
        compiler_params=params(),
        cost_estimate=cost(2 * dests * slots * held * width, 2 * dests * slots * width),
        name="fill",
    )(index, rows, slot_map)


def kind_rows(kind, slots, rows_ref):
    half = slots // 2
    starts = range(kind * half, rows_ref.shape[0], slots)
    return jnp.concatenate([rows_ref[i : i + half, :] for i in starts], axis=0)


def split_rows(slots, rows, out_ref):
    half, features = slots // 2, rows.shape[1] // 2
    parts = []
    for i in range(0, rows.shape[0], half):
        parts += [rows[i : i + half, :features], rows[i : i + half, features:]]
    out_ref[...] = jnp.concatenate(parts, axis=0)


def forward_kernel(slots, rows_ref, gate_ref, up_ref, down_ref, out_ref):
    slot_rows = kind_rows(0, slots, rows_ref)
    gate_pre = jnp.dot(slot_rows, gate_ref[...], preferred_element_type=F32)
    up_pre = jnp.dot(slot_rows, up_ref[...], preferred_element_type=F32)
    hidden = (gate_pre * jax.nn.sigmoid(gate_pre) * up_pre).astype(BF)
    partial_rows = jnp.dot(hidden, down_ref[...], preferred_element_type=F32).astype(BF)
    split_rows(slots, partial_rows, out_ref)


def backward_kernel(slots, rows_ref, gate_ref, up_ref, down_ref, out_ref, hidden_ref, gate_grad_ref, up_grad_ref):
    slot_rows = kind_rows(0, slots, rows_ref)
    scaled = kind_rows(1, slots, rows_ref)
    gate_pre = jnp.dot(slot_rows, gate_ref[...], preferred_element_type=F32)
    up_pre = jnp.dot(slot_rows, up_ref[...], preferred_element_type=F32)
    hidden_grad = lax.dot_general(scaled, down_ref[...], OUTER, preferred_element_type=F32)
    sigmoid_gate = jax.nn.sigmoid(gate_pre)
    active = gate_pre * sigmoid_gate
    gate_pre_grad = (
        hidden_grad * up_pre * sigmoid_gate * (1.0 + gate_pre * (1.0 - sigmoid_gate))
    ).astype(BF)
    up_pre_grad = (hidden_grad * active).astype(BF)
    hidden_ref[...] = (active * up_pre).astype(BF)
    gate_grad_ref[...] = gate_pre_grad
    up_grad_ref[...] = up_pre_grad
    back_rows = (
        lax.dot_general(gate_pre_grad, gate_ref[...], OUTER, preferred_element_type=F32)
        + lax.dot_general(up_pre_grad, up_ref[...], OUTER, preferred_element_type=F32)
    ).astype(BF)
    split_rows(slots, back_rows, out_ref)


def expert_call(kernel, rows, slabs, kept, name, slots, steps=4):
    count, width = rows.shape
    units = slabs[0].shape[1]
    chunk = lambda size, columns: pl.BlockSpec((size // steps, columns), lambda i: (i, 0))
    return pl.pallas_call(
        functools.partial(kernel, slots),
        grid=(steps,),
        in_specs=[chunk(count, width)] + [whole(a) for a in slabs],
        out_specs=[chunk(count, width // 2)] + [chunk(count // 2, units)] * kept,
        out_shape=[jax.ShapeDtypeStruct((count, width // 2), BF)]
        + [jax.ShapeDtypeStruct((count // 2, units), BF)] * kept,
        compiler_params=params(),
        cost_estimate=cost(3 * count * units * width, 3 * count * width + 6 * units * width, count * units),
        name=name,
    )(rows, *slabs)


def slab_grad_kernel(slots, rows_ref, hidden_ref, gate_grad_ref, up_grad_ref, gate_out, up_out, down_out):
    slot_rows, scaled = kind_rows(0, slots, rows_ref), kind_rows(1, slots, rows_ref)
    gate_out[...] = lax.dot_general(slot_rows, gate_grad_ref[...], INNER, preferred_element_type=F32).astype(BF)
    up_out[...] = lax.dot_general(slot_rows, up_grad_ref[...], INNER, preferred_element_type=F32).astype(BF)
    down_out[...] = lax.dot_general(hidden_ref[...], scaled, INNER, preferred_element_type=F32).astype(BF)


def slab_grads(rows, hidden, gate_pre_grad, up_pre_grad, slots, steps=4):
    count, width = rows.shape
    units = hidden.shape[1]
    part = width // steps
    return pl.pallas_call(
        functools.partial(slab_grad_kernel, slots),
        grid=(steps,),
        in_specs=[pl.BlockSpec((count, part), lambda i: (0, i)), whole(hidden), whole(hidden), whole(hidden)],
        out_specs=[pl.BlockSpec((part, units), lambda i: (i, 0))] * 2
        + [pl.BlockSpec((units, part), lambda i: (0, i))],
        out_shape=[jax.ShapeDtypeStruct((width, units), BF)] * 2 + [jax.ShapeDtypeStruct((units, width), BF)],
        compiler_params=params(),
        cost_estimate=cost(3 * count * units * width, 2 * count * width + 6 * units * width),
        name="slab_grads",
    )(rows, hidden, gate_pre_grad, up_pre_grad)


def by_row(table, slots, count):
    repeat = (iota((table.shape[0], count), 1) // slots == iota((table.shape[0], count), 0)).astype(BF)
    return lax.dot_general(table.astype(BF), repeat, INNER, preferred_element_type=F32)


def prepare_kernel(here, slots, rows_ref, code_ref, weight_ref, high_ref, low_ref, mask_ref, grad_ref):
    held, count = high_ref.shape
    half = grad_ref.shape[1]
    slot = (iota((held, count), 1) % slots).astype(F32)
    chosen = by_row(code_ref[...], slots, count) == slot
    weight = weight_ref[...]
    high = weight.astype(BF).astype(F32)
    mask_ref[...] = jnp.where(chosen, 1.0, 0.0).astype(BF)
    high_ref[...] = jnp.where(chosen, by_row(high, slots, count), 0.0).astype(BF)
    low_ref[...] = jnp.where(chosen, by_row(weight - high, slots, count), 0.0).astype(BF)
    for k in range(0, held, 2 * here):
        rows = rows_ref[k : k + 2 * here, : 2 * half].astype(F32)[here:]
        grad_ref[k : k + 2 * here, :] = jnp.concatenate([rows[:, :half], rows[:, half:]], axis=0).astype(BF)


def prepare(rows, code, weight, here, slots):
    held, wide = rows.shape
    count = code.shape[0] * slots
    return pl.pallas_call(
        functools.partial(prepare_kernel, here, slots),
        out_shape=[jax.ShapeDtypeStruct((held, count), BF)] * 3
        + [jax.ShapeDtypeStruct((held, (wide - EXTRA) // 2), BF)],
        compiler_params=params(),
        name="prepare",
    )(rows, code, weight)


def store_blocks(index_ref, total_ref, outs, columns):
    size = outs[0].shape[0]
    for k, out_ref in zip(STEPS, outs):
        at = pl.multiple_of((index_ref[0, 0] + k) % len(outs) * size, size)
        out_ref[:, columns] = total_ref[pl.ds(at, size), :].astype(BF)


def layer_sum_kernel(slots, index_ref, back_ref, rows_ref, code_ref, ids_ref, expert_ref, high_ref, low_ref, *refs):
    *outs, total_ref, gate_ref, dots_ref = refs
    held = high_ref.shape[0]
    top = ids_ref.shape[0]
    dests = code_ref.shape[0]
    part = back_ref.shape[1]
    half = outs[0].shape[1] - EXTRA
    step = pl.program_id(0)

    @pl.when(step == 0)
    def _():
        dots_ref[...] = jnp.zeros_like(dots_ref)

    back = back_ref[...]
    total_ref[...] = jnp.dot(high_ref[...], back, preferred_element_type=F32) + jnp.dot(
        low_ref[...], back, preferred_element_type=F32
    )
    store_blocks(index_ref, total_ref, outs, pl.ds(pl.multiple_of(step * part, part), part))
    dots_ref[...] += lax.dot_general(back, rows_ref[...], OUTER, preferred_element_type=F32)

    @pl.when(step == pl.num_programs(0) - 1)
    def _():
        chosen = code_ref[...][:, None, :] == iota((dests, slots, held), 1).astype(F32)
        by_dest = jnp.sum(jnp.where(chosen, dots_ref[...].reshape(dests, slots, held), 0.0), axis=1)
        dest_expert = expert_ref[...][:, :1]
        rows = [
            jnp.sum(jnp.where(ids_ref[j : j + 1, :] == dest_expert, by_dest, 0.0), axis=0, keepdims=True)
            for j in range(top)
        ]
        gate = jnp.concatenate(rows + [jnp.zeros((EXTRA - top, held), F32)], axis=0)
        gate_ref[...] = lax.dot_general(gate.astype(BF), identity(EXTRA), INNER, preferred_element_type=F32)
        store_blocks(index_ref, gate_ref, outs, slice(half, half + EXTRA))


def layer_sums(index, returned, rows, code, ids, dest_expert, high, low, slots, steps=2):
    count, half = returned.shape
    held = rows.shape[0]
    size = held // len(STEPS)
    part = half // steps
    chunk = lambda size: pl.BlockSpec((size, part), lambda i: (0, i))
    return pl.pallas_call(
        functools.partial(layer_sum_kernel, slots),
        grid=(steps,),
        in_specs=[pl.BlockSpec(memory_space=pltpu.SMEM), chunk(count), chunk(held)]
        + [whole(a) for a in (code, ids, dest_expert, high, low)],
        out_specs=[pl.BlockSpec((size, half + EXTRA), lambda i: (0, 0))] * len(STEPS),
        out_shape=[jax.ShapeDtypeStruct((size, half + EXTRA), BF)] * len(STEPS),
        scratch_shapes=[
            pltpu.VMEM((held, part), F32),
            pltpu.VMEM((held, EXTRA), F32),
            pltpu.VMEM((count, held), F32),
        ],
        compiler_params=params(),
        cost_estimate=cost(6 * count * held * half, 2 * count * half),
        name="layer_sums",
    )(index, returned, rows, code, ids, dest_expert, high, low)


def token_sum_kernel(index_ref, back_ref, mask_ref, *refs):
    *outs, total_ref = refs
    total_ref[...] = jnp.dot(mask_ref[...], back_ref[...], preferred_element_type=F32)
    store_blocks(index_ref, total_ref, outs, slice(None))


def token_sums(index, returned, mask, steps=2):
    count, half = returned.shape
    held = mask.shape[0]
    size = held // len(STEPS)
    part = half // steps
    chunk = lambda size: pl.BlockSpec((size, part), lambda i: (0, i))
    return pl.pallas_call(
        token_sum_kernel,
        grid=(steps,),
        in_specs=[pl.BlockSpec(memory_space=pltpu.SMEM), chunk(count), whole(mask)],
        out_specs=[chunk(size)] * len(STEPS),
        out_shape=[jax.ShapeDtypeStruct((size, half), BF)] * len(STEPS),
        scratch_shapes=[pltpu.VMEM((held, part), F32)],
        compiler_params=params(),
        cost_estimate=cost(2 * count * held * half, 2 * count * half),
        name="token_sums",
    )(index, returned, mask)


def sum_blocks(sums):
    n = lax.axis_size("zhi")
    total = sums[0].astype(F32)
    for rows, step in zip(sums[1:], STEPS[1:]):
        moved = lax.ppermute(rows, "zhi", [(i, (i + step) % n) for i in range(n)])
        total += moved.astype(F32)
    return total


def body(tokens, out_grad, experts, gate_values, slot_map, gate_weight, up_weight, down_weight):
    here, width = tokens.shape
    top = experts.shape[1]
    groups, members = slot_map.shape
    blocks = len(STEPS)
    near = members // blocks
    per_group = members // 2
    capacity = 2 * here * top // (groups * per_group)
    dests = groups * near
    slots = 2 * blocks * capacity

    own = pack(tokens, out_grad, experts.T, gate_values.T)
    rows = lax.all_gather(own, "zhi", axis=0, tiled=True)

    def exchange(rows):
        columns = rows.shape[1]
        moved = lax.all_to_all(
            rows.reshape(dests, slots, columns), SPREAD, split_axis=0, concat_axis=0, tiled=True
        )
        return moved.reshape(dests * slots, columns)

    after = lax.optimization_barrier
    index = lax.axis_index("zhi").astype(jnp.int32).reshape(1, 1)
    slabs = (gate_weight[0], up_weight[0], down_weight[0])
    sent, code, weight, ids, dest_expert = fill(index, rows, slot_map, dests, here, top, slots, width)
    arrived = exchange(sent)
    (partial_out,) = expert_call(forward_kernel, arrived, slabs, 0, "forward", slots)
    partial_out, arrived, rows = after((partial_out, arrived, rows))
    partial_back = exchange(partial_out)
    back_rows, hidden, gate_pre_grad, up_pre_grad = expert_call(
        backward_kernel, arrived, slabs, 3, "backward", slots
    )
    grad_gate, grad_up, grad_down = slab_grads(arrived, hidden, gate_pre_grad, up_pre_grad, slots)
    high, low, mask, grads = prepare(rows, code, weight, here, slots)
    back_rows, partial_back, high, low, mask, grads, grad_gate, grad_up, grad_down = after(
        (back_rows, partial_back, high, low, mask, grads, grad_gate, grad_up, grad_down)
    )
    back_back = exchange(back_rows)
    layer = sum_blocks(layer_sums(index, partial_back, grads, code, ids, dest_expert, high, low, slots))
    back_back, layer = after((back_back, layer))
    token = sum_blocks(token_sums(index, back_back, mask))

    half = width // 2
    layer_out = jnp.concatenate([layer[:here, :half], layer[here:, :half]], axis=1).astype(BF)
    gate_grad = layer[:here, half : half + top] + layer[here:, half : half + top]
    token_grad = jnp.concatenate([token[:here], token[here:]], axis=1).astype(BF)
    return (layer_out, token_grad, gate_grad, grad_gate[None], grad_up[None], grad_down[None])


def solution(mesh):
    groups, members = mesh.devices.shape
    axes = ("y", "core", "zhi", "zlo", "x")
    fine = Mesh(mesh.devices.reshape(groups // 2, 2, members // 8, 2, 4), axes)
    two, three = P(axes, None), P(axes, None, None)
    return jax.shard_map(
        body,
        mesh=fine,
        in_specs=(two, two, two, two, P(), three, three, three),
        out_specs=(two, two, two, three, three, three),
        check_vma=False,
    )
```

```python
import functools

import jax
import jax.numpy as jnp
from jax import lax
from jax.experimental import pallas as pl
from jax.experimental.pallas import tpu as pltpu
from jax.sharding import Mesh
from jax.sharding import PartitionSpec as P

BF = jnp.bfloat16
F32 = jnp.float32
SPREAD = ("zlo", "x", "y", "core")
EXTRA = 128
STEPS = (0, 1, 2, 3)
INNER = (((0,), (0,)), ((), ()))
OUTER = (((1,), (1,)), ((), ()))
VMEM_LIMIT = 48 * 1024 * 1024


def iota(shape, dim):
    return lax.broadcasted_iota(jnp.int32, shape, dim)


def identity(n):
    return (iota((n, n), 0) == iota((n, n), 1)).astype(BF)


def whole(a):
    return pl.BlockSpec(a.shape, lambda i: (0, 0))


def cost(flops, moved, special=0):
    return pl.CostEstimate(flops=flops, bytes_accessed=moved, transcendentals=special)


def params(limit=VMEM_LIMIT):
    return pltpu.CompilerParams(vmem_limit_bytes=limit)


def make_tables(here, top, slots, info, dest_expert, code_ref, weight_ref, ids_ref):
    dests, held = code_ref.shape
    info_t = lax.dot_general(identity(EXTRA), info, OUTER, preferred_element_type=F32)
    ids = info_t[:top]
    gates = info_t[top : 2 * top] + info_t[2 * top : 3 * top] + info_t[3 * top : 4 * top]
    names = jnp.zeros((dests, held), F32)
    weight = jnp.zeros((dests, held), F32)
    for j in range(top):
        matched = ids[j : j + 1] == dest_expert
        names += jnp.where(matched, 1.0, 0.0)
        weight += jnp.where(matched, gates[j : j + 1], 0.0)
    first, later = iota((held, held), 0), iota((held, held), 1)
    before = ((first // here == later // here) & (first < later)).astype(BF)
    rank = jnp.dot(names.astype(BF), before, preferred_element_type=F32)
    row = iota((dests, held), 1)
    blocks = held // (2 * here)
    place = row // (2 * here) + row // here % 2 * (slots // 2)
    code_ref[...] = jnp.where(names > 0.0, rank * float(blocks) + place.astype(F32), -1.0)
    weight_ref[...] = weight
    ids_ref[...] = ids


def dest_experts(index, slot_map, dests):
    groups, members = slot_map.shape
    near = dests // groups
    row = (iota((dests, groups), 0) % groups == iota((dests, groups), 1)).astype(BF)
    held = jnp.dot(row, slot_map.astype(F32).astype(BF), preferred_element_type=F32)
    column = index * near + iota((dests, members), 0) // groups
    held = jnp.sum(jnp.where(iota((dests, members), 1) == column, held, 0.0), axis=1, keepdims=True)
    first = iota((dests, 1), 0) % groups * (members // 2)
    return (held.astype(jnp.int32) // 2 + first).astype(F32)


def pack_kernel(index_ref, tokens_ref, out_grad_ref, experts_ref, gates_ref, map_ref, out_ref, expert_ref):
    here, width = tokens_ref.shape
    top = experts_ref.shape[0]
    gates = gates_ref[...]
    high = gates.astype(BF)
    middle = (gates - high.astype(F32)).astype(BF)
    low = (gates - high.astype(F32) - middle.astype(F32)).astype(BF)
    extra = jnp.zeros((here, EXTRA), F32)
    for k, part in enumerate((experts_ref[...].astype(F32).astype(BF), high, middle, low)):
        place = (iota((top, EXTRA), 0) + k * top == iota((top, EXTRA), 1)).astype(BF)
        extra += lax.dot_general(part, place, INNER, preferred_element_type=F32)
    held = dest_experts(index_ref[0, 0], map_ref[...], expert_ref.shape[0])
    expert_ref[...] = jnp.broadcast_to(held, expert_ref.shape)
    rows = [tokens_ref[...].astype(F32), out_grad_ref[...].astype(F32)]
    out_ref[:, :width] = jnp.concatenate(rows, axis=0).astype(BF)
    out_ref[:, width:] = jnp.concatenate([extra, extra], axis=0).astype(BF)


def pack(index, tokens, out_grad, experts_t, gates_t, slot_map, dests):
    here, width = tokens.shape
    return pl.pallas_call(
        pack_kernel,
        in_specs=[pl.BlockSpec(memory_space=pltpu.SMEM)] + [pl.BlockSpec(memory_space=pltpu.VMEM)] * 5,
        out_shape=[
            jax.ShapeDtypeStruct((2 * here, width + EXTRA), BF),
            jax.ShapeDtypeStruct((dests, 128), F32),
        ],
        name="pack",
    )(index, tokens, out_grad, experts_t, gates_t, slot_map)


def fill_kernel(here, top, slots, rows_ref, expert_ref, out_ref, code_ref, weight_ref, ids_ref):
    held, width = rows_ref.shape[0], out_ref.shape[1]
    step = pl.program_id(0)

    @pl.when(step == 0)
    def _():
        make_tables(here, top, slots, rows_ref[:, width:], expert_ref[...][:, :1], code_ref, weight_ref, ids_ref)

    part = out_ref.shape[0] // slots
    at = pl.ds(pl.multiple_of(step * part, part), part)
    chosen = code_ref[at, :][:, None, :] == iota((part, slots, held), 1).astype(F32)
    scale = jnp.where(iota((part, held), 1) // here % 2 == 0, 1.0, weight_ref[at, :])
    scaled = jnp.where(chosen, scale[:, None, :], 0.0).reshape(part * slots, held)
    scale = jnp.sum(scaled, axis=1, keepdims=True)
    mask = jnp.where(chosen, 1.0, 0.0).reshape(part * slots, held).astype(BF)
    raw = jnp.dot(mask, rows_ref[:, :width], preferred_element_type=F32)
    out_ref[...] = (scale * raw).astype(BF)


def fill(rows, dest_expert, here, top, slots, width, steps=2):
    held = rows.shape[0]
    dests = dest_expert.shape[0]
    part = dests // steps * slots
    tables = [(dests, held), (dests, held), (top, held)]
    return pl.pallas_call(
        functools.partial(fill_kernel, here, top, slots),
        grid=(steps,),
        in_specs=[whole(rows), whole(dest_expert)],
        out_specs=[pl.BlockSpec((part, width), lambda i: (i, 0))]
        + [pl.BlockSpec(shape, lambda i: (0, 0)) for shape in tables],
        out_shape=[jax.ShapeDtypeStruct((dests * slots, width), BF)]
        + [jax.ShapeDtypeStruct(shape, F32) for shape in tables],
        compiler_params=params(),
        cost_estimate=cost(2 * dests * slots * held * width, 2 * dests * slots * width),
        name="fill",
    )(rows, dest_expert)


def kind_rows(kind, slots, rows_ref):
    half = slots // 2
    starts = range(kind * half, rows_ref.shape[0], slots)
    return jnp.concatenate([rows_ref[i : i + half, :] for i in starts], axis=0)


def split_rows(slots, rows, out_ref):
    half, features = slots // 2, rows.shape[1] // 2
    parts = []
    for i in range(0, rows.shape[0], half):
        parts += [rows[i : i + half, :features], rows[i : i + half, features:]]
    out_ref[...] = jnp.concatenate(parts, axis=0)


def forward_kernel(slots, rows_ref, gate_ref, up_ref, down_ref, out_ref):
    slot_rows = kind_rows(0, slots, rows_ref)
    gate_pre = jnp.dot(slot_rows, gate_ref[...], preferred_element_type=F32)
    up_pre = jnp.dot(slot_rows, up_ref[...], preferred_element_type=F32)
    hidden = (gate_pre * jax.nn.sigmoid(gate_pre) * up_pre).astype(BF)
    partial_rows = jnp.dot(hidden, down_ref[...], preferred_element_type=F32).astype(BF)
    split_rows(slots, partial_rows, out_ref)


def backward_kernel(slots, rows_ref, gate_ref, up_ref, down_ref, out_ref, hidden_ref, gate_grad_ref, up_grad_ref):
    slot_rows = kind_rows(0, slots, rows_ref)
    scaled = kind_rows(1, slots, rows_ref)
    gate_pre = jnp.dot(slot_rows, gate_ref[...], preferred_element_type=F32)
    up_pre = jnp.dot(slot_rows, up_ref[...], preferred_element_type=F32)
    hidden_grad = lax.dot_general(scaled, down_ref[...], OUTER, preferred_element_type=F32)
    sigmoid_gate = jax.nn.sigmoid(gate_pre)
    active = gate_pre * sigmoid_gate
    gate_pre_grad = (
        hidden_grad * up_pre * sigmoid_gate * (1.0 + gate_pre * (1.0 - sigmoid_gate))
    ).astype(BF)
    up_pre_grad = (hidden_grad * active).astype(BF)
    hidden_ref[...] = (active * up_pre).astype(BF)
    gate_grad_ref[...] = gate_pre_grad
    up_grad_ref[...] = up_pre_grad
    back_rows = (
        lax.dot_general(gate_pre_grad, gate_ref[...], OUTER, preferred_element_type=F32)
        + lax.dot_general(up_pre_grad, up_ref[...], OUTER, preferred_element_type=F32)
    ).astype(BF)
    split_rows(slots, back_rows, out_ref)


def expert_call(kernel, rows, slabs, kept, name, slots, steps=4):
    count, width = rows.shape
    units = slabs[0].shape[1]
    chunk = lambda size, columns: pl.BlockSpec((size // steps, columns), lambda i: (i, 0))
    return pl.pallas_call(
        functools.partial(kernel, slots),
        grid=(steps,),
        in_specs=[chunk(count, width)] + [whole(a) for a in slabs],
        out_specs=[chunk(count, width // 2)] + [chunk(count // 2, units)] * kept,
        out_shape=[jax.ShapeDtypeStruct((count, width // 2), BF)]
        + [jax.ShapeDtypeStruct((count // 2, units), BF)] * kept,
        compiler_params=params(),
        cost_estimate=cost(3 * count * units * width, 3 * count * width + 6 * units * width, count * units),
        name=name,
    )(rows, *slabs)


def slab_grad_kernel(slots, rows_ref, hidden_ref, gate_grad_ref, up_grad_ref, gate_out, up_out, down_out):
    slot_rows, scaled = kind_rows(0, slots, rows_ref), kind_rows(1, slots, rows_ref)
    gate_out[...] = lax.dot_general(slot_rows, gate_grad_ref[...], INNER, preferred_element_type=F32).astype(BF)
    up_out[...] = lax.dot_general(slot_rows, up_grad_ref[...], INNER, preferred_element_type=F32).astype(BF)
    down_out[...] = lax.dot_general(hidden_ref[...], scaled, INNER, preferred_element_type=F32).astype(BF)


def slab_grads(rows, hidden, gate_pre_grad, up_pre_grad, slots, steps=4):
    count, width = rows.shape
    units = hidden.shape[1]
    part = width // steps
    return pl.pallas_call(
        functools.partial(slab_grad_kernel, slots),
        grid=(steps,),
        in_specs=[pl.BlockSpec((count, part), lambda i: (0, i)), whole(hidden), whole(hidden), whole(hidden)],
        out_specs=[pl.BlockSpec((part, units), lambda i: (i, 0))] * 2
        + [pl.BlockSpec((units, part), lambda i: (0, i))],
        out_shape=[jax.ShapeDtypeStruct((width, units), BF)] * 2 + [jax.ShapeDtypeStruct((units, width), BF)],
        compiler_params=params(),
        cost_estimate=cost(3 * count * units * width, 2 * count * width + 6 * units * width),
        name="slab_grads",
    )(rows, hidden, gate_pre_grad, up_pre_grad)


def by_row(table, slots, count):
    repeat = (iota((table.shape[0], count), 1) // slots == iota((table.shape[0], count), 0)).astype(BF)
    return lax.dot_general(table.astype(BF), repeat, INNER, preferred_element_type=F32)


def prepare_kernel(here, slots, rows_ref, code_ref, weight_ref, high_ref, low_ref, mask_ref, grad_ref):
    held, count = high_ref.shape
    half = grad_ref.shape[1]
    slot = (iota((held, count), 1) % slots).astype(F32)
    chosen = by_row(code_ref[...], slots, count) == slot
    weight = weight_ref[...]
    high = weight.astype(BF).astype(F32)
    mask_ref[...] = jnp.where(chosen, 1.0, 0.0).astype(BF)
    high_ref[...] = jnp.where(chosen, by_row(high, slots, count), 0.0).astype(BF)
    low_ref[...] = jnp.where(chosen, by_row(weight - high, slots, count), 0.0).astype(BF)
    for k in range(0, held, 2 * here):
        rows = rows_ref[k : k + 2 * here, : 2 * half].astype(F32)[here:]
        grad_ref[k : k + 2 * here, :] = jnp.concatenate([rows[:, :half], rows[:, half:]], axis=0).astype(BF)


def prepare(rows, code, weight, here, slots):
    held, wide = rows.shape
    count = code.shape[0] * slots
    return pl.pallas_call(
        functools.partial(prepare_kernel, here, slots),
        out_shape=[jax.ShapeDtypeStruct((held, count), BF)] * 3
        + [jax.ShapeDtypeStruct((held, (wide - EXTRA) // 2), BF)],
        compiler_params=params(),
        name="prepare",
    )(rows, code, weight)


def store_blocks(index_ref, total_ref, outs, columns):
    size = outs[0].shape[0]
    for k, out_ref in zip(STEPS, outs):
        at = pl.multiple_of((index_ref[0, 0] + k) % len(outs) * size, size)
        out_ref[:, columns] = total_ref[pl.ds(at, size), :].astype(BF)


def layer_sum_kernel(slots, index_ref, back_ref, rows_ref, code_ref, ids_ref, expert_ref, high_ref, low_ref, *refs):
    *outs, total_ref, gate_ref, dots_ref = refs
    held = high_ref.shape[0]
    top = ids_ref.shape[0]
    dests = code_ref.shape[0]
    part = back_ref.shape[1]
    half = outs[0].shape[1] - EXTRA
    step = pl.program_id(0)

    @pl.when(step == 0)
    def _():
        dots_ref[...] = jnp.zeros_like(dots_ref)

    back = back_ref[...]
    total_ref[...] = jnp.dot(high_ref[...], back, preferred_element_type=F32) + jnp.dot(
        low_ref[...], back, preferred_element_type=F32
    )
    store_blocks(index_ref, total_ref, outs, pl.ds(pl.multiple_of(step * part, part), part))
    dots_ref[...] += lax.dot_general(back, rows_ref[...], OUTER, preferred_element_type=F32)

    @pl.when(step == pl.num_programs(0) - 1)
    def _():
        chosen = code_ref[...][:, None, :] == iota((dests, slots, held), 1).astype(F32)
        by_dest = jnp.sum(jnp.where(chosen, dots_ref[...].reshape(dests, slots, held), 0.0), axis=1)
        dest_expert = expert_ref[...][:, :1]
        rows = [
            jnp.sum(jnp.where(ids_ref[j : j + 1, :] == dest_expert, by_dest, 0.0), axis=0, keepdims=True)
            for j in range(top)
        ]
        gate = jnp.concatenate(rows + [jnp.zeros((EXTRA - top, held), F32)], axis=0)
        gate_ref[...] = lax.dot_general(gate.astype(BF), identity(EXTRA), INNER, preferred_element_type=F32)
        store_blocks(index_ref, gate_ref, outs, slice(half, half + EXTRA))


def layer_sums(index, returned, rows, code, ids, dest_expert, high, low, slots, steps=2):
    count, half = returned.shape
    held = rows.shape[0]
    size = held // len(STEPS)
    part = half // steps
    chunk = lambda size: pl.BlockSpec((size, part), lambda i: (0, i))
    return pl.pallas_call(
        functools.partial(layer_sum_kernel, slots),
        grid=(steps,),
        in_specs=[pl.BlockSpec(memory_space=pltpu.SMEM), chunk(count), chunk(held)]
        + [whole(a) for a in (code, ids, dest_expert, high, low)],
        out_specs=[pl.BlockSpec((size, half + EXTRA), lambda i: (0, 0))] * len(STEPS),
        out_shape=[jax.ShapeDtypeStruct((size, half + EXTRA), BF)] * len(STEPS),
        scratch_shapes=[
            pltpu.VMEM((held, part), F32),
            pltpu.VMEM((held, EXTRA), F32),
            pltpu.VMEM((count, held), F32),
        ],
        compiler_params=params(20 * 1024 * 1024),
        cost_estimate=cost(6 * count * held * half, 2 * count * half),
        name="layer_sums",
    )(index, returned, rows, code, ids, dest_expert, high, low)


def token_sum_kernel(index_ref, back_ref, mask_ref, *refs):
    *outs, total_ref = refs
    total_ref[...] = jnp.dot(mask_ref[...], back_ref[...], preferred_element_type=F32)
    store_blocks(index_ref, total_ref, outs, slice(None))


def token_sums(index, returned, mask, steps=1):
    count, half = returned.shape
    held = mask.shape[0]
    size = held // len(STEPS)
    part = half // steps
    chunk = lambda size: pl.BlockSpec((size, part), lambda i: (0, i))
    return pl.pallas_call(
        token_sum_kernel,
        grid=(steps,),
        in_specs=[pl.BlockSpec(memory_space=pltpu.SMEM), chunk(count), whole(mask)],
        out_specs=[chunk(size)] * len(STEPS),
        out_shape=[jax.ShapeDtypeStruct((size, half), BF)] * len(STEPS),
        scratch_shapes=[pltpu.VMEM((held, part), F32)],
        compiler_params=params(20 * 1024 * 1024),
        cost_estimate=cost(2 * count * held * half, 2 * count * half),
        name="token_sums",
    )(index, returned, mask)


def send_blocks(parts):
    n = lax.axis_size("zhi")
    return [
        lax.ppermute(rows, "zhi", [(i, (i + step) % n) for i in range(n)])
        for rows, step in zip(parts, STEPS[1:])
    ]


def add_blocks(own, rest):
    total = own.astype(F32)
    for rows in rest:
        total += rows.astype(F32)
    return total


def body(tokens, out_grad, experts, gate_values, slot_map, gate_weight, up_weight, down_weight):
    here, width = tokens.shape
    top = experts.shape[1]
    groups, members = slot_map.shape
    blocks = len(STEPS)
    near = members // blocks
    per_group = members // 2
    capacity = 2 * here * top // (groups * per_group)
    dests = groups * near
    slots = 2 * blocks * capacity

    index = lax.axis_index("zhi").astype(jnp.int32).reshape(1, 1)
    own, dest_expert = pack(index, tokens, out_grad, experts.T, gate_values.T, slot_map, dests)
    rows = lax.all_gather(own, "zhi", axis=0, tiled=True)

    def exchange(rows):
        columns = rows.shape[1]
        moved = lax.all_to_all(
            rows.reshape(dests, slots, columns), SPREAD, split_axis=0, concat_axis=0, tiled=True
        )
        return moved.reshape(dests * slots, columns)

    after = lax.optimization_barrier
    slabs = (gate_weight[0], up_weight[0], down_weight[0])
    sent, code, weight, ids = fill(rows, dest_expert, here, top, slots, width)
    arrived = exchange(sent)
    (partial_out,) = expert_call(forward_kernel, arrived, slabs, 0, "forward", slots)
    partial_out, arrived, rows = after((partial_out, arrived, rows))
    partial_back = exchange(partial_out)
    back_rows, hidden, gate_pre_grad, up_pre_grad = expert_call(
        backward_kernel, arrived, slabs, 3, "backward", slots
    )
    grad_gate, grad_up, grad_down = slab_grads(arrived, hidden, gate_pre_grad, up_pre_grad, slots)
    high, low, mask, grads = prepare(rows, code, weight, here, slots)
    back_rows, partial_back, high, low, mask, grads, grad_gate, grad_up, grad_down = after(
        (back_rows, partial_back, high, low, mask, grads, grad_gate, grad_up, grad_down)
    )
    back_back = exchange(back_rows)
    own_layer, *layer_parts = layer_sums(index, partial_back, grads, code, ids, dest_expert, high, low, slots)
    layer_rest = send_blocks(layer_parts)
    back_back, own_layer = after((back_back, own_layer))
    own_token, *token_parts = token_sums(index, back_back, mask)
    token_rest = send_blocks(token_parts)
    layer = add_blocks(own_layer, layer_rest)
    token = add_blocks(own_token, token_rest)

    half = width // 2
    layer_out = jnp.concatenate([layer[:here, :half], layer[here:, :half]], axis=1).astype(BF)
    gate_grad = layer[:here, half : half + top] + layer[here:, half : half + top]
    token_grad = jnp.concatenate([token[:here], token[here:]], axis=1).astype(BF)
    return (layer_out, token_grad, gate_grad, grad_gate[None], grad_up[None], grad_down[None])


def solution(mesh):
    groups, members = mesh.devices.shape
    axes = ("y", "core", "zhi", "zlo", "x")
    fine = Mesh(mesh.devices.reshape(groups // 2, 2, members // 8, 2, 4), axes)
    two, three = P(axes, None), P(axes, None, None)
    return jax.shard_map(
        body,
        mesh=fine,
        in_specs=(two, two, two, two, P(), three, three, three),
        out_specs=(two, two, two, three, three, three),
        check_vma=False,
    )
```

```python
import functools

import jax
import jax.numpy as jnp
from jax import lax
from jax.experimental import pallas as pl
from jax.experimental.pallas import tpu as pltpu
from jax.sharding import Mesh
from jax.sharding import PartitionSpec as P

BF = jnp.bfloat16
F32 = jnp.float32
SPREAD = ("y", "core", "zlo", "x")
EXTRA = 128
STEPS = (0, 1, 2, 3)
INNER = (((0,), (0,)), ((), ()))
OUTER = (((1,), (1,)), ((), ()))
VMEM_LIMIT = 48 * 1024 * 1024


def iota(shape, dim):
    return lax.broadcasted_iota(jnp.int32, shape, dim)


def identity(n):
    return (iota((n, n), 0) == iota((n, n), 1)).astype(BF)


def whole(a):
    return pl.BlockSpec(a.shape, lambda i: (0, 0))


def cost(flops, moved, special=0):
    return pl.CostEstimate(flops=flops, bytes_accessed=moved, transcendentals=special)


def params(limit=VMEM_LIMIT):
    return pltpu.CompilerParams(vmem_limit_bytes=limit)


def make_tables(here, top, slots, info, dest_expert, code_ref, weight_ref, ids_ref):
    dests, held = code_ref.shape
    info_t = lax.dot_general(identity(EXTRA), info, OUTER, preferred_element_type=F32)
    ids = info_t[:top]
    gates = info_t[top : 2 * top] + info_t[2 * top : 3 * top] + info_t[3 * top : 4 * top]
    names = jnp.zeros((dests, held), F32)
    weight = jnp.zeros((dests, held), F32)
    for j in range(top):
        matched = ids[j : j + 1] == dest_expert
        names += jnp.where(matched, 1.0, 0.0)
        weight += jnp.where(matched, gates[j : j + 1], 0.0)
    first, later = iota((held, held), 0), iota((held, held), 1)
    before = ((first // here == later // here) & (first < later)).astype(BF)
    rank = jnp.dot(names.astype(BF), before, preferred_element_type=F32)
    row = iota((dests, held), 1)
    blocks = held // (2 * here)
    place = row // (2 * here) + row // here % 2 * (slots // 2)
    code_ref[...] = jnp.where(names > 0.0, rank * float(blocks) + place.astype(F32), -1.0)
    weight_ref[...] = weight
    ids_ref[...] = ids


def dest_experts(index, slot_map, dests):
    groups, members = slot_map.shape
    near = dests // groups
    row = (iota((dests, groups), 0) // near == iota((dests, groups), 1)).astype(BF)
    held = jnp.dot(row, slot_map.astype(F32).astype(BF), preferred_element_type=F32)
    column = index * near + iota((dests, members), 0) % near
    held = jnp.sum(jnp.where(iota((dests, members), 1) == column, held, 0.0), axis=1, keepdims=True)
    first = iota((dests, 1), 0) // near * (members // 2)
    return (held.astype(jnp.int32) // 2 + first).astype(F32)


def pack_kernel(index_ref, tokens_ref, out_grad_ref, experts_ref, gates_ref, map_ref, out_ref, expert_ref):
    here, width = tokens_ref.shape
    top = experts_ref.shape[0]
    gates = gates_ref[...]
    high = gates.astype(BF)
    middle = (gates - high.astype(F32)).astype(BF)
    low = (gates - high.astype(F32) - middle.astype(F32)).astype(BF)
    extra = jnp.zeros((here, EXTRA), F32)
    for k, part in enumerate((experts_ref[...].astype(F32).astype(BF), high, middle, low)):
        place = (iota((top, EXTRA), 0) + k * top == iota((top, EXTRA), 1)).astype(BF)
        extra += lax.dot_general(part, place, INNER, preferred_element_type=F32)
    held = dest_experts(index_ref[0, 0], map_ref[...], expert_ref.shape[0])
    expert_ref[...] = jnp.broadcast_to(held, expert_ref.shape)
    rows = [tokens_ref[...].astype(F32), out_grad_ref[...].astype(F32)]
    out_ref[:, :width] = jnp.concatenate(rows, axis=0).astype(BF)
    out_ref[:, width:] = jnp.concatenate([extra, extra], axis=0).astype(BF)


def pack(index, tokens, out_grad, experts_t, gates_t, slot_map, dests):
    here, width = tokens.shape
    return pl.pallas_call(
        pack_kernel,
        in_specs=[pl.BlockSpec(memory_space=pltpu.SMEM)] + [pl.BlockSpec(memory_space=pltpu.VMEM)] * 5,
        out_shape=[
            jax.ShapeDtypeStruct((2 * here, width + EXTRA), BF),
            jax.ShapeDtypeStruct((dests, 128), F32),
        ],
        name="pack",
    )(index, tokens, out_grad, experts_t, gates_t, slot_map)


def fill_kernel(here, top, slots, rows_ref, expert_ref, out_ref, code_ref, weight_ref, ids_ref):
    held, width = rows_ref.shape[0], out_ref.shape[1]
    step = pl.program_id(0)

    @pl.when(step == 0)
    def _():
        make_tables(here, top, slots, rows_ref[:, width:], expert_ref[...][:, :1], code_ref, weight_ref, ids_ref)

    part = out_ref.shape[0] // slots
    at = pl.ds(pl.multiple_of(step * part, part), part)
    chosen = code_ref[at, :][:, None, :] == iota((part, slots, held), 1).astype(F32)
    scale = jnp.where(iota((part, held), 1) // here % 2 == 0, 1.0, weight_ref[at, :])
    scaled = jnp.where(chosen, scale[:, None, :], 0.0).reshape(part * slots, held)
    scale = jnp.sum(scaled, axis=1, keepdims=True)
    mask = jnp.where(chosen, 1.0, 0.0).reshape(part * slots, held).astype(BF)
    raw = jnp.dot(mask, rows_ref[:, :width], preferred_element_type=F32)
    out_ref[...] = (scale * raw).astype(BF)


def fill(rows, dest_expert, here, top, slots, width, steps=2):
    held = rows.shape[0]
    dests = dest_expert.shape[0]
    part = dests // steps * slots
    tables = [(dests, held), (dests, held), (top, held)]
    return pl.pallas_call(
        functools.partial(fill_kernel, here, top, slots),
        grid=(steps,),
        in_specs=[whole(rows), whole(dest_expert)],
        out_specs=[pl.BlockSpec((part, width), lambda i: (i, 0))]
        + [pl.BlockSpec(shape, lambda i: (0, 0)) for shape in tables],
        out_shape=[jax.ShapeDtypeStruct((dests * slots, width), BF)]
        + [jax.ShapeDtypeStruct(shape, F32) for shape in tables],
        compiler_params=params(),
        cost_estimate=cost(2 * dests * slots * held * width, 2 * dests * slots * width),
        name="fill",
    )(rows, dest_expert)


def kind_rows(kind, slots, rows_ref):
    half = slots // 2
    starts = range(kind * half, rows_ref.shape[0], slots)
    return jnp.concatenate([rows_ref[i : i + half, :] for i in starts], axis=0)


def split_rows(slots, rows, out_ref):
    half, features = slots // 2, rows.shape[1] // 2
    parts = []
    for i in range(0, rows.shape[0], half):
        parts += [rows[i : i + half, :features], rows[i : i + half, features:]]
    out_ref[...] = jnp.concatenate(parts, axis=0)


def forward_kernel(slots, rows_ref, gate_ref, up_ref, down_ref, out_ref):
    slot_rows = kind_rows(0, slots, rows_ref)
    gate_pre = jnp.dot(slot_rows, gate_ref[...], preferred_element_type=F32)
    up_pre = jnp.dot(slot_rows, up_ref[...], preferred_element_type=F32)
    hidden = (gate_pre * jax.nn.sigmoid(gate_pre) * up_pre).astype(BF)
    partial_rows = jnp.dot(hidden, down_ref[...], preferred_element_type=F32).astype(BF)
    split_rows(slots, partial_rows, out_ref)


def backward_kernel(slots, rows_ref, gate_ref, up_ref, down_ref, out_ref, hidden_ref, gate_grad_ref, up_grad_ref):
    slot_rows = kind_rows(0, slots, rows_ref)
    scaled = kind_rows(1, slots, rows_ref)
    gate_pre = jnp.dot(slot_rows, gate_ref[...], preferred_element_type=F32)
    up_pre = jnp.dot(slot_rows, up_ref[...], preferred_element_type=F32)
    hidden_grad = lax.dot_general(scaled, down_ref[...], OUTER, preferred_element_type=F32)
    sigmoid_gate = jax.nn.sigmoid(gate_pre)
    active = gate_pre * sigmoid_gate
    gate_pre_grad = (
        hidden_grad * up_pre * sigmoid_gate * (1.0 + gate_pre * (1.0 - sigmoid_gate))
    ).astype(BF)
    up_pre_grad = (hidden_grad * active).astype(BF)
    hidden_ref[...] = (active * up_pre).astype(BF)
    gate_grad_ref[...] = gate_pre_grad
    up_grad_ref[...] = up_pre_grad
    back_rows = (
        lax.dot_general(gate_pre_grad, gate_ref[...], OUTER, preferred_element_type=F32)
        + lax.dot_general(up_pre_grad, up_ref[...], OUTER, preferred_element_type=F32)
    ).astype(BF)
    split_rows(slots, back_rows, out_ref)


def expert_call(kernel, rows, slabs, kept, name, slots, steps=4):
    count, width = rows.shape
    units = slabs[0].shape[1]
    chunk = lambda size, columns: pl.BlockSpec((size // steps, columns), lambda i: (i, 0))
    return pl.pallas_call(
        functools.partial(kernel, slots),
        grid=(steps,),
        in_specs=[chunk(count, width)] + [whole(a) for a in slabs],
        out_specs=[chunk(count, width // 2)] + [chunk(count // 2, units)] * kept,
        out_shape=[jax.ShapeDtypeStruct((count, width // 2), BF)]
        + [jax.ShapeDtypeStruct((count // 2, units), BF)] * kept,
        compiler_params=params(),
        cost_estimate=cost(3 * count * units * width, 3 * count * width + 6 * units * width, count * units),
        name=name,
    )(rows, *slabs)


def slab_grad_kernel(slots, rows_ref, hidden_ref, gate_grad_ref, up_grad_ref, gate_out, up_out, down_out):
    slot_rows, scaled = kind_rows(0, slots, rows_ref), kind_rows(1, slots, rows_ref)
    gate_out[...] = lax.dot_general(slot_rows, gate_grad_ref[...], INNER, preferred_element_type=F32).astype(BF)
    up_out[...] = lax.dot_general(slot_rows, up_grad_ref[...], INNER, preferred_element_type=F32).astype(BF)
    down_out[...] = lax.dot_general(hidden_ref[...], scaled, INNER, preferred_element_type=F32).astype(BF)


def slab_grads(rows, hidden, gate_pre_grad, up_pre_grad, slots, steps=4):
    count, width = rows.shape
    units = hidden.shape[1]
    part = width // steps
    return pl.pallas_call(
        functools.partial(slab_grad_kernel, slots),
        grid=(steps,),
        in_specs=[pl.BlockSpec((count, part), lambda i: (0, i)), whole(hidden), whole(hidden), whole(hidden)],
        out_specs=[pl.BlockSpec((part, units), lambda i: (i, 0))] * 2
        + [pl.BlockSpec((units, part), lambda i: (0, i))],
        out_shape=[jax.ShapeDtypeStruct((width, units), BF)] * 2 + [jax.ShapeDtypeStruct((units, width), BF)],
        compiler_params=params(),
        cost_estimate=cost(3 * count * units * width, 2 * count * width + 6 * units * width),
        name="slab_grads",
    )(rows, hidden, gate_pre_grad, up_pre_grad)


def by_row(table, slots, count):
    repeat = (iota((table.shape[0], count), 1) // slots == iota((table.shape[0], count), 0)).astype(BF)
    return lax.dot_general(table.astype(BF), repeat, INNER, preferred_element_type=F32)


def prepare_kernel(here, slots, rows_ref, code_ref, weight_ref, high_ref, low_ref, mask_ref, grad_ref):
    held, count = high_ref.shape
    half = grad_ref.shape[1]
    slot = (iota((held, count), 1) % slots).astype(F32)
    chosen = by_row(code_ref[...], slots, count) == slot
    weight = weight_ref[...]
    high = weight.astype(BF).astype(F32)
    mask_ref[...] = jnp.where(chosen, 1.0, 0.0).astype(BF)
    high_ref[...] = jnp.where(chosen, by_row(high, slots, count), 0.0).astype(BF)
    low_ref[...] = jnp.where(chosen, by_row(weight - high, slots, count), 0.0).astype(BF)
    for k in range(0, held, 2 * here):
        rows = rows_ref[k : k + 2 * here, : 2 * half].astype(F32)[here:]
        grad_ref[k : k + 2 * here, :] = jnp.concatenate([rows[:, :half], rows[:, half:]], axis=0).astype(BF)


def prepare(rows, code, weight, here, slots):
    held, wide = rows.shape
    count = code.shape[0] * slots
    return pl.pallas_call(
        functools.partial(prepare_kernel, here, slots),
        out_shape=[jax.ShapeDtypeStruct((held, count), BF)] * 3
        + [jax.ShapeDtypeStruct((held, (wide - EXTRA) // 2), BF)],
        compiler_params=params(),
        name="prepare",
    )(rows, code, weight)


def store_blocks(index_ref, total_ref, outs, columns):
    size = outs[0].shape[0]
    for k, out_ref in zip(STEPS, outs):
        at = pl.multiple_of((index_ref[0, 0] + k) % len(outs) * size, size)
        out_ref[:, columns] = total_ref[pl.ds(at, size), :].astype(BF)


def layer_sum_kernel(slots, index_ref, back_ref, rows_ref, code_ref, ids_ref, expert_ref, high_ref, low_ref, *refs):
    *outs, total_ref, gate_ref, dots_ref = refs
    held = high_ref.shape[0]
    top = ids_ref.shape[0]
    dests = code_ref.shape[0]
    part = back_ref.shape[1]
    half = outs[0].shape[1] - EXTRA
    step = pl.program_id(0)

    @pl.when(step == 0)
    def _():
        dots_ref[...] = jnp.zeros_like(dots_ref)

    back = back_ref[...]
    total_ref[...] = jnp.dot(high_ref[...], back, preferred_element_type=F32) + jnp.dot(
        low_ref[...], back, preferred_element_type=F32
    )
    store_blocks(index_ref, total_ref, outs, pl.ds(pl.multiple_of(step * part, part), part))
    dots_ref[...] += lax.dot_general(back, rows_ref[...], OUTER, preferred_element_type=F32)

    @pl.when(step == pl.num_programs(0) - 1)
    def _():
        chosen = code_ref[...][:, None, :] == iota((dests, slots, held), 1).astype(F32)
        by_dest = jnp.sum(jnp.where(chosen, dots_ref[...].reshape(dests, slots, held), 0.0), axis=1)
        dest_expert = expert_ref[...][:, :1]
        rows = [
            jnp.sum(jnp.where(ids_ref[j : j + 1, :] == dest_expert, by_dest, 0.0), axis=0, keepdims=True)
            for j in range(top)
        ]
        gate = jnp.concatenate(rows + [jnp.zeros((EXTRA - top, held), F32)], axis=0)
        gate_ref[...] = lax.dot_general(gate.astype(BF), identity(EXTRA), INNER, preferred_element_type=F32)
        store_blocks(index_ref, gate_ref, outs, slice(half, half + EXTRA))


def layer_sums(index, returned, rows, code, ids, dest_expert, high, low, slots, steps=2):
    count, half = returned.shape
    held = rows.shape[0]
    size = held // len(STEPS)
    part = half // steps
    chunk = lambda size: pl.BlockSpec((size, part), lambda i: (0, i))
    return pl.pallas_call(
        functools.partial(layer_sum_kernel, slots),
        grid=(steps,),
        in_specs=[pl.BlockSpec(memory_space=pltpu.SMEM), chunk(count), chunk(held)]
        + [whole(a) for a in (code, ids, dest_expert, high, low)],
        out_specs=[pl.BlockSpec((size, half + EXTRA), lambda i: (0, 0))] * len(STEPS),
        out_shape=[jax.ShapeDtypeStruct((size, half + EXTRA), BF)] * len(STEPS),
        scratch_shapes=[
            pltpu.VMEM((held, part), F32),
            pltpu.VMEM((held, EXTRA), F32),
            pltpu.VMEM((count, held), F32),
        ],
        compiler_params=params(20 * 1024 * 1024),
        cost_estimate=cost(6 * count * held * half, 2 * count * half),
        name="layer_sums",
    )(index, returned, rows, code, ids, dest_expert, high, low)


def token_sum_kernel(index_ref, back_ref, mask_ref, *refs):
    *outs, total_ref = refs
    total_ref[...] = jnp.dot(mask_ref[...], back_ref[...], preferred_element_type=F32)
    store_blocks(index_ref, total_ref, outs, slice(None))


def token_sums(index, returned, mask, steps=1):
    count, half = returned.shape
    held = mask.shape[0]
    size = held // len(STEPS)
    part = half // steps
    chunk = lambda size: pl.BlockSpec((size, part), lambda i: (0, i))
    return pl.pallas_call(
        token_sum_kernel,
        grid=(steps,),
        in_specs=[pl.BlockSpec(memory_space=pltpu.SMEM), chunk(count), whole(mask)],
        out_specs=[chunk(size)] * len(STEPS),
        out_shape=[jax.ShapeDtypeStruct((size, half), BF)] * len(STEPS),
        scratch_shapes=[pltpu.VMEM((held, part), F32)],
        compiler_params=params(20 * 1024 * 1024),
        cost_estimate=cost(2 * count * held * half, 2 * count * half),
        name="token_sums",
    )(index, returned, mask)


def send_blocks(parts):
    n = lax.axis_size("zhi")
    return [
        lax.ppermute(rows, "zhi", [(i, (i + step) % n) for i in range(n)])
        for rows, step in zip(parts, STEPS[1:])
    ]


def add_blocks(own, rest):
    total = own.astype(F32)
    for rows in rest:
        total += rows.astype(F32)
    return total


def body(tokens, out_grad, experts, gate_values, slot_map, gate_weight, up_weight, down_weight):
    here, width = tokens.shape
    top = experts.shape[1]
    groups, members = slot_map.shape
    blocks = len(STEPS)
    near = members // blocks
    per_group = members // 2
    capacity = 2 * here * top // (groups * per_group)
    dests = groups * near
    slots = 2 * blocks * capacity

    index = lax.axis_index("zhi").astype(jnp.int32).reshape(1, 1)
    own, dest_expert = pack(index, tokens, out_grad, experts.T, gate_values.T, slot_map, dests)
    rows = lax.all_gather(own, "zhi", axis=0, tiled=True)

    def exchange(rows):
        columns = rows.shape[1]
        moved = lax.all_to_all(
            rows.reshape(dests, slots, columns), SPREAD, split_axis=0, concat_axis=0, tiled=True
        )
        return moved.reshape(dests * slots, columns)

    after = lax.optimization_barrier
    slabs = (gate_weight[0], up_weight[0], down_weight[0])
    sent, code, weight, ids = fill(rows, dest_expert, here, top, slots, width)
    arrived = exchange(sent)
    (partial_out,) = expert_call(forward_kernel, arrived, slabs, 0, "forward", slots)
    partial_out, arrived, rows = after((partial_out, arrived, rows))
    partial_back = exchange(partial_out)
    back_rows, hidden, gate_pre_grad, up_pre_grad = expert_call(
        backward_kernel, arrived, slabs, 3, "backward", slots
    )
    grad_gate, grad_up, grad_down = slab_grads(arrived, hidden, gate_pre_grad, up_pre_grad, slots)
    high, low, mask, grads = prepare(rows, code, weight, here, slots)
    back_rows, partial_back, high, low, mask, grads, grad_gate, grad_up, grad_down = after(
        (back_rows, partial_back, high, low, mask, grads, grad_gate, grad_up, grad_down)
    )
    back_back = exchange(back_rows)
    own_layer, *layer_parts = layer_sums(index, partial_back, grads, code, ids, dest_expert, high, low, slots)
    layer_rest = send_blocks(layer_parts)
    back_back, own_layer = after((back_back, own_layer))
    own_token, *token_parts = token_sums(index, back_back, mask)
    token_rest = send_blocks(token_parts)
    layer = add_blocks(own_layer, layer_rest)
    token = add_blocks(own_token, token_rest)

    half = width // 2
    layer_out = jnp.concatenate([layer[:here, :half], layer[here:, :half]], axis=1).astype(BF)
    gate_grad = layer[:here, half : half + top] + layer[here:, half : half + top]
    token_grad = jnp.concatenate([token[:here], token[here:]], axis=1).astype(BF)
    return (layer_out, token_grad, gate_grad, grad_gate[None], grad_up[None], grad_down[None])


def solution(mesh):
    groups, members = mesh.devices.shape
    axes = ("y", "core", "zhi", "zlo", "x")
    fine = Mesh(mesh.devices.reshape(groups // 2, 2, members // 8, 2, 4), axes)
    two, three = P(axes, None), P(axes, None, None)
    return jax.shard_map(
        body,
        mesh=fine,
        in_specs=(two, two, two, two, P(), three, three, three),
        out_specs=(two, two, two, three, three, three),
        check_vma=False,
    )
```

```python
import functools

import jax
import jax.numpy as jnp
from jax import lax
from jax.experimental import pallas as pl
from jax.experimental.pallas import tpu as pltpu
from jax.sharding import Mesh
from jax.sharding import PartitionSpec as P

BF = jnp.bfloat16
F32 = jnp.float32
SPREAD = ("y", "core", "zlo", "x")
EXTRA = 128
STEPS = (0, 2, 1, 3)
INNER = (((0,), (0,)), ((), ()))
OUTER = (((1,), (1,)), ((), ()))
VMEM_LIMIT = 48 * 1024 * 1024


def iota(shape, dim):
    return lax.broadcasted_iota(jnp.int32, shape, dim)


def identity(n):
    return (iota((n, n), 0) == iota((n, n), 1)).astype(BF)


def whole(a):
    return pl.BlockSpec(a.shape, lambda i: (0, 0))


def cost(flops, moved, special=0):
    return pl.CostEstimate(flops=flops, bytes_accessed=moved, transcendentals=special)


def params(limit=VMEM_LIMIT):
    return pltpu.CompilerParams(vmem_limit_bytes=limit)


def make_tables(here, top, slots, info, dest_expert, code_ref, weight_ref, ids_ref):
    dests, held = code_ref.shape
    info_t = lax.dot_general(identity(EXTRA), info, OUTER, preferred_element_type=F32)
    ids = info_t[:top]
    gates = info_t[top : 2 * top] + info_t[2 * top : 3 * top] + info_t[3 * top : 4 * top]
    names = jnp.zeros((dests, held), F32)
    weight = jnp.zeros((dests, held), F32)
    for j in range(top):
        matched = ids[j : j + 1] == dest_expert
        names += jnp.where(matched, 1.0, 0.0)
        weight += jnp.where(matched, gates[j : j + 1], 0.0)
    first, later = iota((held, held), 0), iota((held, held), 1)
    before = ((first // here == later // here) & (first < later)).astype(BF)
    rank = jnp.dot(names.astype(BF), before, preferred_element_type=F32)
    row = iota((dests, held), 1)
    blocks = held // (2 * here)
    place = row // (2 * here) + row // here % 2 * (slots // 2)
    code_ref[...] = jnp.where(names > 0.0, rank * float(blocks) + place.astype(F32), -1.0)
    weight_ref[...] = weight
    ids_ref[...] = ids


def dest_experts(index, slot_map, dests):
    groups, members = slot_map.shape
    near = dests // groups
    row = (iota((dests, groups), 0) // near == iota((dests, groups), 1)).astype(BF)
    held = jnp.dot(row, slot_map.astype(F32).astype(BF), preferred_element_type=F32)
    column = index * near + iota((dests, members), 0) % near
    held = jnp.sum(jnp.where(iota((dests, members), 1) == column, held, 0.0), axis=1, keepdims=True)
    first = iota((dests, 1), 0) // near * (members // 2)
    return (held.astype(jnp.int32) // 2 + first).astype(F32)


def pack_kernel(index_ref, tokens_ref, out_grad_ref, experts_ref, gates_ref, map_ref, out_ref, expert_ref):
    here, width = tokens_ref.shape
    top = experts_ref.shape[0]
    gates = gates_ref[...]
    high = gates.astype(BF)
    middle = (gates - high.astype(F32)).astype(BF)
    low = (gates - high.astype(F32) - middle.astype(F32)).astype(BF)
    extra = jnp.zeros((here, EXTRA), F32)
    for k, part in enumerate((experts_ref[...].astype(F32).astype(BF), high, middle, low)):
        place = (iota((top, EXTRA), 0) + k * top == iota((top, EXTRA), 1)).astype(BF)
        extra += lax.dot_general(part, place, INNER, preferred_element_type=F32)
    held = dest_experts(index_ref[0, 0], map_ref[...], expert_ref.shape[0])
    expert_ref[...] = jnp.broadcast_to(held, expert_ref.shape)
    rows = [tokens_ref[...].astype(F32), out_grad_ref[...].astype(F32)]
    out_ref[:, :width] = jnp.concatenate(rows, axis=0).astype(BF)
    out_ref[:, width:] = jnp.concatenate([extra, extra], axis=0).astype(BF)


def pack(index, tokens, out_grad, experts_t, gates_t, slot_map, dests):
    here, width = tokens.shape
    return pl.pallas_call(
        pack_kernel,
        in_specs=[pl.BlockSpec(memory_space=pltpu.SMEM)] + [pl.BlockSpec(memory_space=pltpu.VMEM)] * 5,
        out_shape=[
            jax.ShapeDtypeStruct((2 * here, width + EXTRA), BF),
            jax.ShapeDtypeStruct((dests, 128), F32),
        ],
        name="pack",
    )(index, tokens, out_grad, experts_t, gates_t, slot_map)


def fill_kernel(here, top, slots, rows_ref, expert_ref, out_ref, code_ref, weight_ref, ids_ref):
    held, width = rows_ref.shape[0], out_ref.shape[1]
    step = pl.program_id(0)

    @pl.when(step == 0)
    def _():
        make_tables(here, top, slots, rows_ref[:, width:], expert_ref[...][:, :1], code_ref, weight_ref, ids_ref)

    part = out_ref.shape[0] // slots
    at = pl.ds(pl.multiple_of(step * part, part), part)
    chosen = code_ref[at, :][:, None, :] == iota((part, slots, held), 1).astype(F32)
    scale = jnp.where(iota((part, held), 1) // here % 2 == 0, 1.0, weight_ref[at, :])
    scaled = jnp.where(chosen, scale[:, None, :], 0.0).reshape(part * slots, held)
    scale = jnp.sum(scaled, axis=1, keepdims=True)
    mask = jnp.where(chosen, 1.0, 0.0).reshape(part * slots, held).astype(BF)
    raw = jnp.dot(mask, rows_ref[:, :width], preferred_element_type=F32)
    out_ref[...] = (scale * raw).astype(BF)


def fill(rows, dest_expert, here, top, slots, width, steps=2):
    held = rows.shape[0]
    dests = dest_expert.shape[0]
    part = dests // steps * slots
    tables = [(dests, held), (dests, held), (top, held)]
    return pl.pallas_call(
        functools.partial(fill_kernel, here, top, slots),
        grid=(steps,),
        in_specs=[whole(rows), whole(dest_expert)],
        out_specs=[pl.BlockSpec((part, width), lambda i: (i, 0))]
        + [pl.BlockSpec(shape, lambda i: (0, 0)) for shape in tables],
        out_shape=[jax.ShapeDtypeStruct((dests * slots, width), BF)]
        + [jax.ShapeDtypeStruct(shape, F32) for shape in tables],
        compiler_params=params(),
        cost_estimate=cost(2 * dests * slots * held * width, 2 * dests * slots * width),
        name="fill",
    )(rows, dest_expert)


def kind_rows(kind, slots, rows_ref):
    half = slots // 2
    starts = range(kind * half, rows_ref.shape[0], slots)
    return jnp.concatenate([rows_ref[i : i + half, :] for i in starts], axis=0)


def split_rows(slots, rows, out_ref):
    half, features = slots // 2, rows.shape[1] // 2
    parts = []
    for i in range(0, rows.shape[0], half):
        parts += [rows[i : i + half, :features], rows[i : i + half, features:]]
    out_ref[...] = jnp.concatenate(parts, axis=0)


def forward_kernel(slots, rows_ref, gate_ref, up_ref, down_ref, out_ref):
    slot_rows = kind_rows(0, slots, rows_ref)
    gate_pre = jnp.dot(slot_rows, gate_ref[...], preferred_element_type=F32)
    up_pre = jnp.dot(slot_rows, up_ref[...], preferred_element_type=F32)
    hidden = (gate_pre * jax.nn.sigmoid(gate_pre) * up_pre).astype(BF)
    partial_rows = jnp.dot(hidden, down_ref[...], preferred_element_type=F32).astype(BF)
    split_rows(slots, partial_rows, out_ref)


def backward_kernel(slots, rows_ref, gate_ref, up_ref, down_ref, out_ref, hidden_ref, gate_grad_ref, up_grad_ref):
    slot_rows = kind_rows(0, slots, rows_ref)
    scaled = kind_rows(1, slots, rows_ref)
    gate_pre = jnp.dot(slot_rows, gate_ref[...], preferred_element_type=F32)
    up_pre = jnp.dot(slot_rows, up_ref[...], preferred_element_type=F32)
    hidden_grad = lax.dot_general(scaled, down_ref[...], OUTER, preferred_element_type=F32)
    sigmoid_gate = jax.nn.sigmoid(gate_pre)
    active = gate_pre * sigmoid_gate
    gate_pre_grad = (
        hidden_grad * up_pre * sigmoid_gate * (1.0 + gate_pre * (1.0 - sigmoid_gate))
    ).astype(BF)
    up_pre_grad = (hidden_grad * active).astype(BF)
    hidden_ref[...] = (active * up_pre).astype(BF)
    gate_grad_ref[...] = gate_pre_grad
    up_grad_ref[...] = up_pre_grad
    back_rows = (
        lax.dot_general(gate_pre_grad, gate_ref[...], OUTER, preferred_element_type=F32)
        + lax.dot_general(up_pre_grad, up_ref[...], OUTER, preferred_element_type=F32)
    ).astype(BF)
    split_rows(slots, back_rows, out_ref)


def expert_call(kernel, rows, slabs, kept, name, slots, steps=4):
    count, width = rows.shape
    units = slabs[0].shape[1]
    chunk = lambda size, columns: pl.BlockSpec((size // steps, columns), lambda i: (i, 0))
    return pl.pallas_call(
        functools.partial(kernel, slots),
        grid=(steps,),
        in_specs=[chunk(count, width)] + [whole(a) for a in slabs],
        out_specs=[chunk(count, width // 2)] + [chunk(count // 2, units)] * kept,
        out_shape=[jax.ShapeDtypeStruct((count, width // 2), BF)]
        + [jax.ShapeDtypeStruct((count // 2, units), BF)] * kept,
        compiler_params=params(),
        cost_estimate=cost(3 * count * units * width, 3 * count * width + 6 * units * width, count * units),
        name=name,
    )(rows, *slabs)


def slab_grad_kernel(slots, rows_ref, hidden_ref, gate_grad_ref, up_grad_ref, gate_out, up_out, down_out):
    slot_rows, scaled = kind_rows(0, slots, rows_ref), kind_rows(1, slots, rows_ref)
    gate_out[...] = lax.dot_general(slot_rows, gate_grad_ref[...], INNER, preferred_element_type=F32).astype(BF)
    up_out[...] = lax.dot_general(slot_rows, up_grad_ref[...], INNER, preferred_element_type=F32).astype(BF)
    down_out[...] = lax.dot_general(hidden_ref[...], scaled, INNER, preferred_element_type=F32).astype(BF)


def slab_grads(rows, hidden, gate_pre_grad, up_pre_grad, slots, steps=4):
    count, width = rows.shape
    units = hidden.shape[1]
    part = width // steps
    return pl.pallas_call(
        functools.partial(slab_grad_kernel, slots),
        grid=(steps,),
        in_specs=[pl.BlockSpec((count, part), lambda i: (0, i)), whole(hidden), whole(hidden), whole(hidden)],
        out_specs=[pl.BlockSpec((part, units), lambda i: (i, 0))] * 2
        + [pl.BlockSpec((units, part), lambda i: (0, i))],
        out_shape=[jax.ShapeDtypeStruct((width, units), BF)] * 2 + [jax.ShapeDtypeStruct((units, width), BF)],
        compiler_params=params(),
        cost_estimate=cost(3 * count * units * width, 2 * count * width + 6 * units * width),
        name="slab_grads",
    )(rows, hidden, gate_pre_grad, up_pre_grad)


def by_row(table, slots, count):
    repeat = (iota((table.shape[0], count), 1) // slots == iota((table.shape[0], count), 0)).astype(BF)
    return lax.dot_general(table.astype(BF), repeat, INNER, preferred_element_type=F32)


def prepare_kernel(here, slots, rows_ref, code_ref, weight_ref, high_ref, low_ref, mask_ref, grad_ref):
    held, count = high_ref.shape
    half = grad_ref.shape[1]
    slot = (iota((held, count), 1) % slots).astype(F32)
    chosen = by_row(code_ref[...], slots, count) == slot
    weight = weight_ref[...]
    high = weight.astype(BF).astype(F32)
    mask_ref[...] = jnp.where(chosen, 1.0, 0.0).astype(BF)
    high_ref[...] = jnp.where(chosen, by_row(high, slots, count), 0.0).astype(BF)
    low_ref[...] = jnp.where(chosen, by_row(weight - high, slots, count), 0.0).astype(BF)
    for k in range(0, held, 2 * here):
        rows = rows_ref[k : k + 2 * here, : 2 * half].astype(F32)[here:]
        grad_ref[k : k + 2 * here, :] = jnp.concatenate([rows[:, :half], rows[:, half:]], axis=0).astype(BF)


def prepare(rows, code, weight, here, slots):
    held, wide = rows.shape
    count = code.shape[0] * slots
    return pl.pallas_call(
        functools.partial(prepare_kernel, here, slots),
        out_shape=[jax.ShapeDtypeStruct((held, count), BF)] * 3
        + [jax.ShapeDtypeStruct((held, (wide - EXTRA) // 2), BF)],
        compiler_params=params(),
        name="prepare",
    )(rows, code, weight)


def store_blocks(index_ref, total_ref, outs, columns):
    size = outs[0].shape[0]
    for k, out_ref in zip(STEPS, outs):
        at = pl.multiple_of((index_ref[0, 0] + k) % len(outs) * size, size)
        out_ref[:, columns] = total_ref[pl.ds(at, size), :].astype(BF)


def layer_sum_kernel(slots, index_ref, back_ref, rows_ref, code_ref, ids_ref, expert_ref, high_ref, low_ref, *refs):
    *outs, total_ref, gate_ref, dots_ref = refs
    held = high_ref.shape[0]
    top = ids_ref.shape[0]
    dests = code_ref.shape[0]
    part = back_ref.shape[1]
    half = outs[0].shape[1] - EXTRA
    step = pl.program_id(0)

    @pl.when(step == 0)
    def _():
        dots_ref[...] = jnp.zeros_like(dots_ref)

    back = back_ref[...]
    total_ref[...] = jnp.dot(high_ref[...], back, preferred_element_type=F32) + jnp.dot(
        low_ref[...], back, preferred_element_type=F32
    )
    store_blocks(index_ref, total_ref, outs, pl.ds(pl.multiple_of(step * part, part), part))
    dots_ref[...] += lax.dot_general(back, rows_ref[...], OUTER, preferred_element_type=F32)

    @pl.when(step == pl.num_programs(0) - 1)
    def _():
        chosen = code_ref[...][:, None, :] == iota((dests, slots, held), 1).astype(F32)
        by_dest = jnp.sum(jnp.where(chosen, dots_ref[...].reshape(dests, slots, held), 0.0), axis=1)
        dest_expert = expert_ref[...][:, :1]
        rows = [
            jnp.sum(jnp.where(ids_ref[j : j + 1, :] == dest_expert, by_dest, 0.0), axis=0, keepdims=True)
            for j in range(top)
        ]
        gate = jnp.concatenate(rows + [jnp.zeros((EXTRA - top, held), F32)], axis=0)
        gate_ref[...] = lax.dot_general(gate.astype(BF), identity(EXTRA), INNER, preferred_element_type=F32)
        store_blocks(index_ref, gate_ref, outs, slice(half, half + EXTRA))


def layer_sums(index, returned, rows, code, ids, dest_expert, high, low, slots, steps=2):
    count, half = returned.shape
    held = rows.shape[0]
    size = held // len(STEPS)
    part = half // steps
    chunk = lambda size: pl.BlockSpec((size, part), lambda i: (0, i))
    return pl.pallas_call(
        functools.partial(layer_sum_kernel, slots),
        grid=(steps,),
        in_specs=[pl.BlockSpec(memory_space=pltpu.SMEM), chunk(count), chunk(held)]
        + [whole(a) for a in (code, ids, dest_expert, high, low)],
        out_specs=[pl.BlockSpec((size, half + EXTRA), lambda i: (0, 0))] * len(STEPS),
        out_shape=[jax.ShapeDtypeStruct((size, half + EXTRA), BF)] * len(STEPS),
        scratch_shapes=[
            pltpu.VMEM((held, part), F32),
            pltpu.VMEM((held, EXTRA), F32),
            pltpu.VMEM((count, held), F32),
        ],
        compiler_params=params(20 * 1024 * 1024),
        cost_estimate=cost(6 * count * held * half, 2 * count * half),
        name="layer_sums",
    )(index, returned, rows, code, ids, dest_expert, high, low)


def token_sum_kernel(index_ref, back_ref, mask_ref, *refs):
    *outs, total_ref = refs
    total_ref[...] = jnp.dot(mask_ref[...], back_ref[...], preferred_element_type=F32)
    store_blocks(index_ref, total_ref, outs, slice(None))


def token_sums(index, returned, mask, steps=1):
    count, half = returned.shape
    held = mask.shape[0]
    size = held // len(STEPS)
    part = half // steps
    chunk = lambda size: pl.BlockSpec((size, part), lambda i: (0, i))
    return pl.pallas_call(
        token_sum_kernel,
        grid=(steps,),
        in_specs=[pl.BlockSpec(memory_space=pltpu.SMEM), chunk(count), whole(mask)],
        out_specs=[chunk(size)] * len(STEPS),
        out_shape=[jax.ShapeDtypeStruct((size, half), BF)] * len(STEPS),
        scratch_shapes=[pltpu.VMEM((held, part), F32)],
        compiler_params=params(20 * 1024 * 1024),
        cost_estimate=cost(2 * count * held * half, 2 * count * half),
        name="token_sums",
    )(index, returned, mask)


def send_blocks(parts):
    n = lax.axis_size("zhi")
    return [
        lax.ppermute(rows, "zhi", [(i, (i + step) % n) for i in range(n)])
        for rows, step in zip(parts, STEPS[1:])
    ]


def add_blocks(own, rest):
    total = own.astype(F32)
    for rows in rest:
        total += rows.astype(F32)
    return total


def body(tokens, out_grad, experts, gate_values, slot_map, gate_weight, up_weight, down_weight):
    here, width = tokens.shape
    top = experts.shape[1]
    groups, members = slot_map.shape
    blocks = len(STEPS)
    near = members // blocks
    per_group = members // 2
    capacity = 2 * here * top // (groups * per_group)
    dests = groups * near
    slots = 2 * blocks * capacity

    index = lax.axis_index("zhi").astype(jnp.int32).reshape(1, 1)
    own, dest_expert = pack(index, tokens, out_grad, experts.T, gate_values.T, slot_map, dests)
    rows = lax.all_gather(own, "zhi", axis=0, tiled=True)

    def exchange(rows):
        columns = rows.shape[1]
        moved = lax.all_to_all(
            rows.reshape(dests, slots, columns), SPREAD, split_axis=0, concat_axis=0, tiled=True
        )
        return moved.reshape(dests * slots, columns)

    after = lax.optimization_barrier
    slabs = (gate_weight[0], up_weight[0], down_weight[0])
    sent, code, weight, ids = fill(rows, dest_expert, here, top, slots, width)
    arrived = exchange(sent)
    (partial_out,) = expert_call(forward_kernel, arrived, slabs, 0, "forward", slots)
    partial_out, arrived, rows = after((partial_out, arrived, rows))
    partial_back = exchange(partial_out)
    back_rows, hidden, gate_pre_grad, up_pre_grad = expert_call(
        backward_kernel, arrived, slabs, 3, "backward", slots
    )
    grad_gate, grad_up, grad_down = slab_grads(arrived, hidden, gate_pre_grad, up_pre_grad, slots)
    high, low, mask, grads = prepare(rows, code, weight, here, slots)
    back_rows, partial_back, high, low, mask, grads, grad_gate, grad_up, grad_down = after(
        (back_rows, partial_back, high, low, mask, grads, grad_gate, grad_up, grad_down)
    )
    back_back = exchange(back_rows)
    own_layer, *layer_parts = layer_sums(index, partial_back, grads, code, ids, dest_expert, high, low, slots)
    layer_rest = send_blocks(layer_parts)
    back_back, own_layer = after((back_back, own_layer))
    own_token, *token_parts = token_sums(index, back_back, mask)
    token_rest = send_blocks(token_parts)
    layer = add_blocks(own_layer, layer_rest)
    token = add_blocks(own_token, token_rest)

    half = width // 2
    layer_out = jnp.concatenate([layer[:here, :half], layer[here:, :half]], axis=1).astype(BF)
    gate_grad = layer[:here, half : half + top] + layer[here:, half : half + top]
    token_grad = jnp.concatenate([token[:here], token[here:]], axis=1).astype(BF)
    return (layer_out, token_grad, gate_grad, grad_gate[None], grad_up[None], grad_down[None])


def solution(mesh):
    groups, members = mesh.devices.shape
    axes = ("y", "core", "zhi", "zlo", "x")
    fine = Mesh(mesh.devices.reshape(groups // 2, 2, members // 8, 2, 4), axes)
    two, three = P(axes, None), P(axes, None, None)
    return jax.shard_map(
        body,
        mesh=fine,
        in_specs=(two, two, two, two, P(), three, three, three),
        out_specs=(two, two, two, three, three, three),
        check_vma=False,
    )
```
